128 devices in a mesh: band: 8 (over y, core), tile: 16 (over x, z).
Axes of the slice: x: 4, y: 4, z: 4, core: 2. Of those that a mesh axis runs over, the one named last changes fastest.
Arguments:
- grid_in: bfloat16 [524288, 227], P(('band', 'tile')), may hold values from -6 to 6
- embed_in: bfloat16 [227, 512], replicated, may hold values from -0.375 to 0.375
- embed_out: bfloat16 [512, 512], replicated, may hold values from -0.25 to 0.25
- mesh_latent: bfloat16 [327680, 512], P(('band', 'tile')), may hold values from -6 to 6
- edge_latent: bfloat16 [524288, 512], P(('band', 'tile')), may hold values from -6 to 6
- enc_w: bfloat16 [3, 512, 512], replicated, may hold values from -0.25 to 0.25
- node_w: bfloat16 [3, 512, 512], replicated, may hold values from -0.25 to 0.25
- proc_w: bfloat16 [4, 512, 512], replicated, may hold values from -0.25 to 0.25
- gains: float32 [3, 512], replicated, may hold values from 0.1 to 1.9
- g2m_src: int32 [128, 128, 16], P(('band', 'tile')), may hold values from 0 to 4095
- g2m_dst: int32 [128, 128, 16], P(('band', 'tile')), may hold values from 0 to 2559
- g2m_count: int32 [128, 128], P(('band', 'tile')), may hold values from 0 to 16, as said below
- halo_rows: int32 [128, 128, 16], P(('band', 'tile')), may hold values from 0 to 2559
- proc_dst: int32 [524288], P(('band', 'tile')), may hold values from 0 to 2559
- proc_src: int32 [524288], P(('band', 'tile')), may hold values from 0 to 4607, as said below
Outputs:
- mesh_out: bfloat16 [327680, 512], P(('band', 'tile'))
- edge_out: bfloat16 [524288, 512], P(('band', 'tile'))
The draws below stay inside these ranges and needn't reach their ends.
Inputs may be any that keep to these rules, and one draw needn't show every extreme that they name: `g2m_count`: every sender has live slots to every receiver, at most 16 from each; some receiver has 16 from each of its senders. `proc_src`: halo slots are read from every device other than the reader itself, and every such slot is read by some edge.
All inputs are finite; a program needn't handle non-finite values.
Results may differ from the reference program's by a relative error of at most 0.007.
Values may be sent and summed in bfloat16 or wider, within the bound.
No kernel may reach another device: no remote copies, remote signals or barrier semaphores. Data moves between devices by JAX's collectives and lax.ppermute only.
A program may use at most 128 MiB of HBM per device.

```python
import jax
import jax.numpy as jnp
from jax import lax

F_IN = 227
L = 512
GN_DEV = 4096
M_DEV = 2560
CAP = 16
HCAP = 16
ME_DEV = 4096
DEVS = 128
BANDS = 8
GRID = 524288
MESH = 327680
MESH_EDGES = 524288


def draw_g2m_count(key, part):
    key = jax.random.fold_in(key, 11)
    first, second, third = jax.random.split(key, 3)
    tiles = DEVS // BANDS
    band_of = jnp.arange(DEVS, dtype=jnp.int32) // tiles
    polar = (band_of == 0) | (band_of == BANDS - 1)
    lower = jax.random.randint(first, (DEVS, DEVS), CAP // 2, CAP * 3 // 4 + 1, dtype=jnp.int32)
    upper = jax.random.randint(second, (DEVS, DEVS), CAP * 3 // 4, CAP + 1, dtype=jnp.int32)
    counts = jnp.where(polar[:, None], upper, lower)
    full_row = jax.random.randint(third, (), 0, DEVS, dtype=jnp.int32)
    is_full = jnp.arange(DEVS, dtype=jnp.int32)[:, None] == full_row
    counts = jnp.where(is_full, jnp.int32(CAP), counts)
    return counts.astype(jnp.int32)


def draw_proc_src(key, part):
    key = jax.random.fold_in(key, 12)
    first, second, third, fourth = jax.random.split(key, 4)
    local = jax.random.randint(first, (DEVS, ME_DEV), 0, 2, dtype=jnp.int32)
    pick = jax.random.randint(second, (DEVS, ME_DEV), 0, DEVS - 1, dtype=jnp.int32)
    slot = jax.random.randint(third, (DEVS, ME_DEV), 0, HCAP, dtype=jnp.int32)
    row = jax.random.randint(fourth, (DEVS, ME_DEV), 0, M_DEV, dtype=jnp.int32)
    position = jnp.arange(ME_DEV, dtype=jnp.int32)[None, :]
    covered = position < (DEVS - 1) * HCAP
    pick = jnp.where(covered, jnp.minimum(position // HCAP, DEVS - 2), pick)
    slot = jnp.where(covered, position % HCAP, slot)
    own = jnp.arange(DEVS, dtype=jnp.int32)[:, None]
    peer = (own + 1 + pick) % DEVS
    halo_index = M_DEV + peer * HCAP + slot
    result = jnp.where(covered | (local == 0), halo_index, row)
    return result.reshape(-1).astype(jnp.int32)


def touch_ends(array, key, least, largest):
    longest = array.shape.index(max(array.shape))
    spots = []
    for shift in (0, 1):
        where = [jax.random.randint(jax.random.fold_in(key, axis), (), 0, length) for axis, length in enumerate(array.shape)]
        where[longest] = (where[longest] + shift) % array.shape[longest]
        spots.append(tuple(where))
    return array.at[spots[0]].set(least).at[spots[1]].set(largest)


def steps_of(stream_key, dims, shards, low, top_value):
    def one(axis_at, parts):
        heights = jax.random.uniform(jax.random.fold_in(jax.random.fold_in(stream_key, 6), axis_at), (parts,), jnp.float32, low / len(shards), top_value / len(shards))
        return jnp.repeat(jnp.exp(heights), dims[axis_at] // parts).reshape((-1,) + (1,) * (len(dims) - axis_at - 1))

    level = one(*shards[0])
    for cut in shards[1:]:
        level = level * one(*cut)
    return level


def noise(rng, extent, scale, limit, cuts=(), kind=jnp.bfloat16):
    entries = jax.random.normal(rng, extent, jnp.float32) * scale
    if len(cuts) > 0:
        entries = steps_of(rng, extent, cuts, -0.22, 0.18) * entries
    return jnp.clip(entries, min=-limit, max=limit).astype(kind)


def setup_inputs(seed: int = 0) -> dict:
    keys = jax.random.split(jax.random.key(seed), 16)
    return {
        "grid_in": noise(keys[0], (GRID, F_IN), 1.0, 6.0, ((0, 128),)),
        "embed_in": noise(keys[1], (F_IN, L), F_IN ** -0.5, 0.375),
        "embed_out": noise(keys[2], (L, L), L ** -0.5, 0.25),
        "mesh_latent": noise(keys[3], (MESH, L), 1.0, 6.0, ((0, 128),)),
        "edge_latent": noise(keys[4], (MESH_EDGES, L), 1.0, 6.0, ((0, 128),)),
        "enc_w": noise(keys[5], (3, L, L), L ** -0.5, 0.25),
        "node_w": noise(keys[6], (3, L, L), L ** -0.5, 0.25),
        "proc_w": noise(keys[7], (4, L, L), L ** -0.5, 0.25),
        "gains": jnp.clip(1.0 + 0.18 * jax.random.normal(keys[8], (3, L), jnp.float32), 0.1, 1.9),
        "g2m_src": touch_ends(jax.random.randint(keys[9], (DEVS, DEVS, CAP), 0, GN_DEV), jax.random.fold_in(keys[9], 1), 0, GN_DEV - 1).astype(jnp.int32),
        "g2m_dst": touch_ends(jax.random.randint(keys[10], (DEVS, DEVS, CAP), 0, M_DEV), jax.random.fold_in(keys[10], 1), 0, M_DEV - 1).astype(jnp.int32),
        "g2m_count": draw_g2m_count(jax.random.fold_in(keys[15], 71), 0),
        "halo_rows": touch_ends(jax.random.randint(keys[12], (DEVS, DEVS, HCAP), 0, M_DEV), jax.random.fold_in(keys[12], 1), 0, M_DEV - 1).astype(jnp.int32),
        "proc_dst": touch_ends(jax.random.randint(keys[13], (MESH_EDGES,), 0, M_DEV), jax.random.fold_in(keys[13], 1), 0, M_DEV - 1).astype(jnp.int32),
        "proc_src": draw_proc_src(jax.random.fold_in(keys[15], 71), 0),
    }


def layer_norm(value, gain):
    mean = lax.optimization_barrier(jnp.mean(value, axis=-1, keepdims=True))
    centred = value - mean
    variance = lax.optimization_barrier(jnp.mean(centred * centred, axis=-1, keepdims=True))
    return centred / jnp.sqrt(variance + 1e-05) * gain

def embed_block(rows, embed_in, embed_out, gain):
    hidden = jax.nn.silu(jnp.dot(rows, embed_in, preferred_element_type=jnp.float32)).astype(jnp.bfloat16)
    return layer_norm(jnp.dot(hidden, embed_out, preferred_element_type=jnp.float32), gain).astype(jnp.bfloat16)

def reference(grid_in, embed_in, embed_out, mesh_latent, edge_latent, enc_w, node_w, proc_w, gains, g2m_src, g2m_dst, g2m_count, halo_rows, proc_dst, proc_src):
    grid_blocks = grid_in.reshape(DEVS, GN_DEV, F_IN)
    grid_latent = lax.map(lambda rows: embed_block(rows, embed_in, embed_out, gains[0]), grid_blocks)
    mesh_blocks = mesh_latent.reshape(DEVS, M_DEV, L)
    src_by_recv = jnp.swapaxes(g2m_src, 0, 1)
    senders = jnp.arange(DEVS, dtype=jnp.int32)[:, None]

    def encode(item):
        own, src_q, dst_q, count_q = item
        received = grid_latent[senders, src_q].reshape(DEVS * CAP, L)
        mesh_proj = jnp.dot(own, enc_w[1], preferred_element_type=jnp.float32)
        dst_flat = dst_q.reshape(-1)
        edge_hidden = jax.nn.silu(jnp.dot(received, enc_w[0], preferred_element_type=jnp.float32) + mesh_proj[dst_flat]).astype(jnp.bfloat16)
        message = jnp.dot(edge_hidden, enc_w[2], preferred_element_type=jnp.float32)
        live = (jnp.arange(CAP, dtype=jnp.int32)[None, :] < count_q[:, None]).reshape(-1, 1)
        message = jnp.where(live, message, jnp.float32(0.0))
        aggregate = jnp.zeros((M_DEV, L), jnp.float32).at[dst_flat].add(message).astype(jnp.bfloat16)
        node_hidden = jax.nn.silu(jnp.dot(own, node_w[0], preferred_element_type=jnp.float32) + jnp.dot(aggregate, node_w[1], preferred_element_type=jnp.float32)).astype(jnp.bfloat16)
        update = layer_norm(jnp.dot(node_hidden, node_w[2], preferred_element_type=jnp.float32), gains[1])
        return (own.astype(jnp.float32) + update).astype(jnp.bfloat16)
    mesh_new = lax.map(encode, (mesh_blocks, src_by_recv, g2m_dst, g2m_count))
    halo_by_recv = jnp.swapaxes(halo_rows, 0, 1)
    edge_blocks = edge_latent.reshape(DEVS, ME_DEV, L)

    def process(item):
        own, halo_q, edges, dst_q, src_q = item
        halo = mesh_new[senders, halo_q].reshape(DEVS * HCAP, L)
        table = jnp.concatenate([own, halo], axis=0)
        receiver = own[dst_q]
        sender = table[src_q]
        pre = jnp.dot(edges, proc_w[0], preferred_element_type=jnp.float32) + jnp.dot(receiver, proc_w[1], preferred_element_type=jnp.float32) + jnp.dot(sender, proc_w[2], preferred_element_type=jnp.float32)
        hidden = jax.nn.silu(pre).astype(jnp.bfloat16)
        update = layer_norm(jnp.dot(hidden, proc_w[3], preferred_element_type=jnp.float32), gains[2])
        return (edges.astype(jnp.float32) + update).astype(jnp.bfloat16)
    edge_new = lax.map(process, (mesh_new, halo_by_recv, edge_blocks, proc_dst.reshape(DEVS, ME_DEV), proc_src.reshape(DEVS, ME_DEV)))
    return (mesh_new.reshape(MESH, L), edge_new.reshape(MESH_EDGES, L))
```

```python
import functools

import jax
import jax.numpy as jnp
from jax import lax
from jax.experimental import pallas as pl
from jax.experimental.pallas import tpu as pltpu
from jax.sharding import PartitionSpec as P

F32 = jnp.float32
BF16 = jnp.bfloat16
VMEM = pl.BlockSpec(memory_space=pltpu.VMEM)
SMEM = pl.BlockSpec(memory_space=pltpu.SMEM)
PARAMS = pltpu.CompilerParams(vmem_limit_bytes=52 * 2**20)
UNROLL = 32


def dot(a, b):
    return jnp.dot(a, b, preferred_element_type=F32)


def silu(v):
    half = 0.5 * v
    return half + half * jnp.tanh(half)


def norm(value, gain):
    mean = jnp.mean(value, axis=-1, keepdims=True)
    centred = value - mean
    variance = jnp.mean(centred * centred, axis=-1, keepdims=True)
    return centred * lax.rsqrt(variance + 1e-05) * gain


def put_rows(table, start, value):
    rows, width = value.shape
    parts = -(-width // 128)
    for part in range(parts):
        top = min(width, part * 128 + 128)
        table[pl.ds(start * parts + part, rows, stride=parts), : top - part * 128] = value[
            :, part * 128 : top
        ]


def get_part(table, start, rows, part, parts):
    return table[pl.ds(start * parts + part, rows, stride=parts), :]


def get_rows(table, start, rows, parts):
    return jnp.concatenate(
        [get_part(table, start, rows, part, parts) for part in range(parts)], axis=1
    )


def copy_rows(index, table, target, start, base, rows, parts):
    @pl.loop(0, rows // UNROLL)
    def _(block):
        for inner in range(UNROLL):
            row = block * UNROLL + inner
            source = pl.multiple_of(index[start + row], parts)
            target[pl.ds(pl.multiple_of((base + row) * parts, parts), parts), :] = table[
                pl.ds(source, parts), :
            ]


def pick_grid(index, grid, out, table, picked):
    rows, width = grid.shape
    slots = out.shape[0]
    step = 128

    @pl.loop(0, rows // step)
    def _(block):
        at = pl.multiple_of(block * step, step)
        put_rows(table, at, grid[pl.ds(at, step), :].astype(F32))

    @pl.loop(0, slots // step)
    def _(block):
        at = pl.multiple_of(block * step, step)
        copy_rows(index, table, picked, at, at, step, 2)
        value = get_rows(picked, at, step, 2)
        out[pl.ds(at, step), :] = value[:, :width].astype(BF16)


def mesh_side(index, mesh, w_mesh, w_own, out, own, table):
    rows = mesh.shape[0]
    slots = out.shape[0] // 4
    step = 256

    @pl.loop(0, rows // step)
    def _(block):
        at = pl.multiple_of(block * step, step)
        value = mesh[pl.ds(at, step), :]
        put_rows(table, at, dot(value, w_mesh[...]))
        own[pl.ds(at, step), :] = dot(value, w_own[...])

    copy_rows(index, table, out, 0, 0, slots, 4)


def encode(
    halo_index, rows_in, target, mesh_term, own, mesh, embed_in, embed_out, enc_w, node_w, gains,
    mesh_out, halo_out, hidden, table, picked,
):
    slots, width = rows_in.shape
    mesh_rows = mesh.shape[0]
    step = 256

    @pl.loop(0, slots // step)
    def _(block):
        at = pl.multiple_of(block * step, step)
        first = silu(dot(rows_in[pl.ds(at, step), :], embed_in[...])).astype(BF16)
        latent = norm(dot(first, embed_out[...]), gains[0:1, :]).astype(BF16)
        pre = dot(latent, enc_w[0]) + get_rows(mesh_term, at, step, 4)
        hidden[pl.ds(at, step), :] = silu(pre).astype(BF16)

    block_rows = 640

    @pl.loop(0, mesh_rows // block_rows)
    def _(block):
        at = pl.multiple_of(block * block_rows, block_rows)
        row = lax.broadcasted_iota(jnp.int32, (block_rows, slots), 0) + at
        mask = jnp.where(row == target[...], F32(1.0), F32(0.0)).astype(BF16)
        summed = dot(mask, hidden[...]).astype(BF16)
        aggregate = dot(summed, enc_w[2]).astype(BF16)
        node = silu(own[pl.ds(at, block_rows), :] + dot(aggregate, node_w[1])).astype(BF16)
        update = norm(dot(node, node_w[2]), gains[1:2, :])
        new = (mesh[pl.ds(at, block_rows), :].astype(F32) + update).astype(BF16)
        mesh_out[pl.ds(at, block_rows), :] = new
        put_rows(table, at, new.astype(F32))

    halo_slots = halo_out.shape[0]
    step = 128

    @pl.loop(0, halo_slots // step)
    def _(block):
        at = pl.multiple_of(block * step, step)
        copy_rows(halo_index, table, picked, at, at, step, 4)
        halo_out[pl.ds(at, step), :] = get_rows(picked, at, step, 4).astype(BF16)


def local_terms(dst, src, mesh, proc_w, edges, out, receivers, senders, picked):
    rows = mesh.shape[0]
    block_rows = edges.shape[0]
    step = 256
    grid_step = pl.program_id(0)

    @pl.when(grid_step == 0)
    def _():
        @pl.loop(0, rows // step)
        def _(block):
            at = pl.multiple_of(block * step, step)
            value = mesh[pl.ds(at, step), :]
            put_rows(receivers, at, dot(value, proc_w[1]))
            put_rows(senders, at, dot(value, proc_w[2]))

        senders[pl.ds(rows * 4, 8), :] = jnp.zeros((8, 128), F32)

    start = grid_step * block_rows

    @pl.loop(0, block_rows // UNROLL)
    def _(block):
        for inner in range(UNROLL):
            row = block * UNROLL + inner
            one = pl.multiple_of(dst[start + row], 4)
            two = pl.multiple_of(src[start + row], 4)
            picked[pl.ds(pl.multiple_of(row * 4, 4), 4), :] = (
                receivers[pl.ds(one, 4), :] + senders[pl.ds(two, 4), :]
            )

    out[...] = dot(edges[...], proc_w[0]) + get_rows(picked, 0, block_rows, 4)


def edge_update(src, halo, proc_w, edges, local, gains, out, senders, picked):
    rows = halo.shape[0]
    block_rows = edges.shape[0]
    step = 256
    grid_step = pl.program_id(0)

    @pl.when(grid_step == 0)
    def _():
        @pl.loop(0, rows // step)
        def _(block):
            at = pl.multiple_of(block * step, step)
            put_rows(senders, at, dot(halo[pl.ds(at, step), :], proc_w[2]))

        senders[pl.ds(rows * 4, 8), :] = jnp.zeros((8, 128), F32)

    copy_rows(src, senders, picked, grid_step * block_rows, 0, block_rows, 4)
    pre = local[...] + get_rows(picked, 0, block_rows, 4)
    hidden = silu(pre).astype(BF16)
    update = norm(dot(hidden, proc_w[3]), gains[2:3, :])
    out[...] = (edges[...].astype(F32) + update).astype(BF16)


def shards(
    grid_in,
    embed_in,
    embed_out,
    mesh_latent,
    edge_latent,
    enc_w,
    node_w,
    proc_w,
    gains,
    g2m_src,
    g2m_dst,
    g2m_count,
    halo_rows,
    proc_dst,
    proc_src,
):
    axes = ("band", "tile")
    peers = lax.axis_size("band") * lax.axis_size("tile")
    grid_rows, features = grid_in.shape
    mesh_rows, width = mesh_latent.shape
    edges = edge_latent.shape[0]
    cap = g2m_src.shape[2]
    halo_cap = halo_rows.shape[2]
    slots = peers * cap
    halo_slots = peers * halo_cap
    parts = width // 128

    def full(rows, columns, dtype):
        return jax.ShapeDtypeStruct((rows, columns), dtype)

    def cost(flops, moved):
        return pl.CostEstimate(flops=flops, bytes_accessed=moved, transcendentals=0)

    outgoing = pl.pallas_call(
        pick_grid,
        out_shape=full(slots, features, BF16),
        in_specs=[SMEM, VMEM],
        out_specs=VMEM,
        scratch_shapes=[pltpu.VMEM((grid_rows * 2, 128), F32), pltpu.VMEM((slots * 2, 128), F32)],
        compiler_params=PARAMS,
        name="pick_grid",
    )(g2m_src[0].reshape(-1) * 2, grid_in)
    arrived = lax.all_to_all(
        outgoing.reshape(peers, cap, features), axes, split_axis=0, concat_axis=0, tiled=True
    ).reshape(slots, features)

    dst_flat = g2m_dst[0].reshape(-1)
    mesh_term, own = pl.pallas_call(
        mesh_side,
        out_shape=(full(slots * parts, 128, F32), full(mesh_rows, width, F32)),
        in_specs=[SMEM, VMEM, VMEM, VMEM],
        out_specs=(VMEM, VMEM),
        scratch_shapes=[pltpu.VMEM((mesh_rows * parts, 128), F32)],
        compiler_params=PARAMS,
        cost_estimate=cost(10**10, 2 * 10**7),
        name="mesh_side",
    )(dst_flat * parts, mesh_latent, enc_w[1], node_w[0])

    live = (jnp.arange(cap, dtype=jnp.int32)[None, :] < g2m_count[0][:, None]).reshape(-1)
    target = jnp.where(live, dst_flat, -1).reshape(1, slots)
    mesh_new, halo_out = pl.pallas_call(
        encode,
        out_shape=(full(mesh_rows, width, BF16), full(halo_slots, width, BF16)),
        in_specs=[SMEM] + [VMEM] * 10,
        out_specs=(VMEM, VMEM),
        scratch_shapes=[
            pltpu.VMEM((slots, width), BF16),
            pltpu.VMEM((mesh_rows * parts, 128), F32),
            pltpu.VMEM((halo_slots * parts, 128), F32),
        ],
        compiler_params=PARAMS,
        name="encode",
    )(
        halo_rows[0].reshape(-1) * parts, arrived, target, mesh_term, own, mesh_latent,
        embed_in, embed_out, enc_w, node_w, gains,
    )
    halo_in = lax.all_to_all(
        halo_out.reshape(peers, halo_cap, width), axes, split_axis=0, concat_axis=0, tiled=True
    ).reshape(halo_slots, width)

    block_rows = 512
    block = pl.BlockSpec((block_rows, width), lambda i, *_: (i, 0))
    picked = pltpu.VMEM((block_rows * parts, 128), F32)
    remote = proc_src >= mesh_rows
    local = pl.pallas_call(
        local_terms,
        out_shape=full(edges, width, F32),
        grid=(edges // block_rows,),
        in_specs=[SMEM, SMEM, VMEM, VMEM, block],
        out_specs=block,
        scratch_shapes=[
            pltpu.VMEM((mesh_rows * parts, 128), F32),
            pltpu.VMEM((mesh_rows * parts + 8, 128), F32),
            picked,
        ],
        compiler_params=PARAMS,
        cost_estimate=cost(2 * 10**10, 4 * 10**7),
        name="local_terms",
    )(
        proc_dst * parts,
        jnp.where(remote, mesh_rows, proc_src) * parts,
        mesh_new,
        proc_w,
        edge_latent,
    )
    edge_new = pl.pallas_call(
        edge_update,
        out_shape=full(edges, width, BF16),
        grid=(edges // block_rows,),
        in_specs=[SMEM, VMEM, VMEM, block, block, VMEM],
        out_specs=block,
        scratch_shapes=[pltpu.VMEM((halo_slots * parts + 8, 128), F32), picked],
        compiler_params=PARAMS,
        name="edge_update",
    )(
        jnp.where(remote, proc_src - mesh_rows, halo_slots) * parts,
        halo_in,
        proc_w,
        edge_latent,
        local,
        gains,
    )
    return (mesh_new, edge_new)


def solution(mesh):
    rows = P(("band", "tile"), None)
    slots = P(("band", "tile"), None, None)
    flat = P(("band", "tile"))
    in_specs = (
        rows, P(), P(), rows, rows, P(), P(), P(), P(), slots, slots, rows, slots, flat, flat,
    )
    return jax.shard_map(
        shards, mesh=mesh, in_specs=in_specs, out_specs=(rows, rows), check_vma=False
    )
```

```python
import jax
import jax.numpy as jnp
from jax import lax
from jax.experimental import pallas as pl
from jax.experimental.pallas import tpu as pltpu
from jax.sharding import PartitionSpec as P

F32 = jnp.float32
BF16 = jnp.bfloat16
VMEM = pl.BlockSpec(memory_space=pltpu.VMEM)
SMEM = pl.BlockSpec(memory_space=pltpu.SMEM)
ANY = pl.BlockSpec(memory_space=pl.ANY)
STEP = 256


def params(mebibytes):
    return pltpu.CompilerParams(vmem_limit_bytes=mebibytes * 2**20)


def in_hbm(array):
    return pltpu.with_memory_space_constraint(array, pltpu.HBM)


def dot(a, b):
    return jnp.dot(a, b, preferred_element_type=F32)


def silu(v):
    half = 0.5 * v
    return half + half * jnp.tanh(half)


def norm(value, gain):
    mean = jnp.mean(value, axis=-1, keepdims=True)
    centred = value - mean
    variance = jnp.mean(centred * centred, axis=-1, keepdims=True)
    return centred * lax.rsqrt(variance + 1e-05) * gain


def put_rows(table, start, value):
    rows, width = value.shape
    parts = width // 128
    for part in range(parts):
        table[pl.ds(start * parts + part, rows, stride=parts), :] = value[
            :, part * 128 : part * 128 + 128
        ]


def get_rows(table, start, rows, parts):
    return jnp.concatenate(
        [table[pl.ds(start * parts + part, rows, stride=parts), :] for part in range(parts)],
        axis=1,
    )


def slot_index(index, start, inner, scale):
    cap = index.shape[0]
    peer = start // cap + inner // cap
    return pl.multiple_of(index[inner % cap, peer] * scale, scale)


def pick_rows(at, table, target, base, rows, parts):
    for inner in range(rows):
        target[pl.ds(base * parts + inner * parts, parts), :] = table[pl.ds(at(inner), parts), :]


def pick_grid(index_in, grid_in, out, index, grid, table, picked, turned, index_sem, sems):
    features, rows = grid.shape
    slots = out.shape[0]
    step = STEP * 2

    def grid_copy(part):
        columns = pl.ds(pl.multiple_of(part * step, step), step)
        return pltpu.make_async_copy(grid_in.at[:, columns], grid.at[:, columns], sems.at[part])

    for part in range(rows // step):
        grid_copy(part).start()
    index_copy = pltpu.make_async_copy(index_in, index, index_sem)
    index_copy.start()

    @pl.loop(0, rows // STEP)
    def _(block):
        @pl.when(block % 2 == 0)
        def _():
            grid_copy(block // 2).wait()

        at = pl.multiple_of(block * STEP, STEP)
        turned[pl.ds(0, features), :] = grid[:, pl.ds(at, STEP)]
        put_rows(table, at, turned[...].T.astype(F32))

    index_copy.wait()
    step = 64

    @pl.loop(0, slots // step)
    def _(block):
        at = pl.multiple_of(block * step, step)
        pick_rows(lambda inner: slot_index(index, at, inner, 2), table, picked, at, step, 2)
        out[pl.ds(at, step), :] = get_rows(picked, at, step, 2)[:, :features].astype(BF16)


def piece(ref, part, rows):
    return ref.at[pl.ds(pl.multiple_of(part * rows, rows), rows)]


def mesh_side(
    dst, halo, mesh, enc_w, node_w,
    term_out, own_out, halo_out, folded_out,
    table, copies, picked, picked_too, own, terms, halves, latents, w_enc, w_node, sems,
):
    rows = mesh.shape[0]
    slots = halo_out.shape[0]
    step = 512
    chunks = rows // step
    weights = [
        pltpu.make_async_copy(enc_w.at[pl.ds(1, 2)], w_enc, sems.at[0]),
        pltpu.make_async_copy(node_w.at[pl.ds(0, 2)], w_node, sems.at[1]),
    ]
    for copy in weights:
        copy.start()

    def latent_copy(part):
        return pltpu.make_async_copy(
            piece(mesh, part, step), piece(latents, part, step), sems.at[2 + part]
        )

    for part in range(chunks):
        latent_copy(part).start()
    for copy in weights:
        copy.wait()

    @pl.loop(0, chunks)
    def _(block):
        at = pl.multiple_of(block * step, step)
        latent_copy(block).wait()
        value = latents[pl.ds(at, step), :]
        put_rows(table, at, dot(value, w_enc[0]))
        put_rows(own, at, dot(value, w_node[0]))
        put_rows(copies, at, value.astype(F32))

    outs = [pltpu.make_async_copy(own, own_out, sems.at[0])]
    outs[0].start()
    folded_out[...] = dot(w_enc[1], w_node[1]).astype(BF16)
    step = 64
    parts = 4
    span = slots // parts
    for part in range(parts):

        @pl.loop(part * span // step, (part + 1) * span // step)
        def _(block):
            at = pl.multiple_of(block * step, step)
            pick_rows(lambda inner: slot_index(dst, at, inner, 4), table, picked_too, at, step, 4)
            pick_rows(lambda inner: slot_index(halo, at, inner, 4), copies, picked, at, step, 4)
            terms[pl.ds(at, step), :] = get_rows(picked_too, at, step, 4).astype(BF16)
            halves[pl.ds(at, step), :] = get_rows(picked, at, step, 4).astype(BF16)

        outs.append(
            pltpu.make_async_copy(
                piece(terms, part, span), piece(term_out, part, span), sems.at[2 + part]
            )
        )
        outs[-1].start()
    outs.append(pltpu.make_async_copy(halves, halo_out, sems.at[1]))
    outs[-1].start()
    for copy in outs:
        copy.wait()


def node_update(pre, own, w_out, gain):
    return (own.astype(F32) + norm(dot(silu(pre).astype(BF16), w_out), gain)).astype(BF16)


def encode(
    target, halo, rows_in, mesh_term, own, own_halo, embed_in, embed_out, enc_w, folded, node_w,
    gains, sums_out, halo_out,
    sums, terms, first, second, halves, w_grid, w_message, w_out, halo_rows, sems,
):
    slots = rows_in.shape[0]
    mesh_rows = own.shape[0]
    blocks = slots // STEP
    copies = [
        pltpu.make_async_copy(enc_w.at[0], w_grid, sems.at[0]),
        pltpu.make_async_copy(folded, w_message, sems.at[1]),
        pltpu.make_async_copy(mesh_term, terms, sems.at[2]),
        pltpu.make_async_copy(own, sums.at[pl.ds(0, mesh_rows)], sems.at[3]),
        pltpu.make_async_copy(node_w.at[2], w_out, sems.at[4]),
        pltpu.make_async_copy(own_halo, halves, sems.at[5]),
    ]
    for copy in copies:
        copy.start()
    sums[pl.ds(mesh_rows, 8), :] = jnp.zeros((8, 128), F32)
    for copy in copies[:3]:
        copy.wait()

    def message(block, into):
        at = pl.multiple_of(block * STEP, STEP)
        hidden = silu(dot(rows_in[pl.ds(at, STEP), :], embed_in[...])).astype(BF16)
        latent = norm(dot(hidden, embed_out[...]), gains[0:1, :]).astype(BF16)
        pre = dot(latent, w_grid[...]) + terms[pl.ds(at, STEP), :].astype(F32)
        put_rows(into, 0, dot(silu(pre).astype(BF16), w_message[...]))

    def scatter(block, source):
        for inner in range(STEP):
            row = pl.ds(slot_index(target, block * STEP, inner, 4), 4)
            sums[row, :] = sums[row, :] + source[pl.ds(inner * 4, 4), :]

    message(0, first)
    copies[3].wait()

    @pl.loop(0, blocks // 2 - 1)
    def _(pair):
        message(pair * 2 + 1, second)
        scatter(pair * 2, first)
        message(pair * 2 + 2, first)
        scatter(pair * 2 + 1, second)

    message(blocks - 1, second)
    scatter(blocks - 2, first)
    scatter(blocks - 1, second)
    sums_copy = pltpu.make_async_copy(sums.at[pl.ds(0, mesh_rows)], sums_out, sems.at[3])
    sums_copy.start()
    for copy in copies[4:]:
        copy.wait()

    def pick(block, into):
        pick_rows(lambda inner: slot_index(halo, block * STEP, inner, 4), sums, into, 0, STEP, 4)

    def update(block, source):
        at = pl.multiple_of(block * STEP, STEP)
        halo_rows[pl.ds(at, STEP), :] = node_update(
            get_rows(source, 0, STEP, 4), halves[pl.ds(at, STEP), :], w_out[...], gains[1:2, :]
        )

    pick(0, first)

    def halo_copy(pair):
        return pltpu.make_async_copy(
            piece(halo_rows, pair, STEP * 2), piece(halo_out, pair, STEP * 2), sems.at[6 + pair]
        )

    @pl.loop(0, blocks // 2)
    def _(pair):
        pick(pair * 2 + 1, second)
        update(pair * 2, first)
        pick(jnp.minimum(pair * 2 + 2, blocks - 1), first)
        update(pair * 2 + 1, second)
        halo_copy(pair).start()

    sums_copy.wait()
    for pair in range(blocks // 2):
        halo_copy(pair).wait()


def local_terms(
    dst, src, sums_in, mesh, node_w, proc_w, gains, edges_in, mesh_out, out,
    sums, latents, edges, new, local, w_node, w_proc, receivers, senders, picked, sems, edge_sems,
):
    rows = mesh.shape[0]
    step = 512
    chunks = rows // step
    edge_chunks = edges.shape[0] // step
    weights = [
        pltpu.make_async_copy(node_w.at[2], w_node, sems.at[0]),
        pltpu.make_async_copy(proc_w.at[pl.ds(0, 3)], w_proc, sems.at[1]),
    ]

    def sums_copy(part):
        return pltpu.make_async_copy(
            piece(sums_in, part, step * 4), piece(sums, part, step * 4), sems.at[2 + part]
        )

    def latent_copy(part):
        return pltpu.make_async_copy(
            piece(mesh, part, step), piece(latents, part, step), sems.at[2 + chunks + part]
        )

    def new_copy(part):
        return pltpu.make_async_copy(
            piece(new, part, step), piece(mesh_out, part, step), sems.at[2 + part]
        )

    def edge_copy(part):
        return pltpu.make_async_copy(
            piece(edges_in, part, step), piece(edges, part, step), edge_sems.at[0, part]
        )

    def local_copy(part):
        return pltpu.make_async_copy(
            piece(local, part, step), piece(out, part, step), edge_sems.at[1, part]
        )

    for copy in weights:
        copy.start()
    for part in range(chunks):
        sums_copy(part).start()
        latent_copy(part).start()
    for part in range(edge_chunks):
        edge_copy(part).start()
    senders[pl.ds(rows * 4, 8), :] = jnp.zeros((8, 128), F32)
    for copy in weights:
        copy.wait()

    @pl.loop(0, chunks)
    def _(block):
        at = pl.multiple_of(block * step, step)
        sums_copy(block).wait()
        latent_copy(block).wait()
        value = node_update(
            get_rows(sums, at, step, 4), latents[pl.ds(at, step), :], w_node[...], gains[1:2, :]
        )
        new[pl.ds(at, step), :] = value
        put_rows(receivers, at, dot(value, w_proc[1]))
        put_rows(senders, at, dot(value, w_proc[2]))
        new_copy(block).start()

    @pl.loop(0, edge_chunks)
    def _(block):
        start = pl.multiple_of(block * step, step)
        edge_copy(block).wait()

        @pl.loop(0, step // 32)
        def _(group):
            for inner in range(32):
                row = group * 32 + inner
                one = pl.multiple_of(dst[start + row], 4)
                two = pl.multiple_of(src[start + row], 4)
                picked[pl.ds(pl.multiple_of(row * 4, 4), 4), :] = (
                    receivers[pl.ds(one, 4), :] + senders[pl.ds(two, 4), :]
                )

        here = pl.ds(start, step)
        value = dot(edges[here, :], w_proc[0]) + get_rows(picked, 0, step, 4)
        local[here, :] = value.astype(BF16)
        local_copy(block).start()

    for part in range(chunks):
        new_copy(part).wait()
    for part in range(edge_chunks):
        local_copy(part).wait()


def edge_update(
    src, halo, proc_w, edges_in, local_in, gains, out,
    w_proc, edges, local, new, senders, first, second, sems, edge_sems,
):
    rows = halo.shape[0]
    step = 512
    chunks = rows // step
    edge_chunks = edges.shape[0] // step
    last = src.shape[0] // STEP - 1
    weights = pltpu.make_async_copy(proc_w.at[pl.ds(2, 2)], w_proc, sems.at[0])

    def edge_copy(part):
        return pltpu.make_async_copy(
            piece(edges_in, part, step), piece(edges, part, step), edge_sems.at[0, part]
        )

    def local_copy(part):
        return pltpu.make_async_copy(
            piece(local_in, part, step), piece(local, part, step), edge_sems.at[1, part]
        )

    def new_copy(part):
        return pltpu.make_async_copy(
            piece(new, part, step), piece(out, part, step), edge_sems.at[0, part]
        )

    weights.start()
    for part in range(edge_chunks):
        local_copy(part).start()
        edge_copy(part).start()
    senders[pl.ds(rows * 4, 8), :] = jnp.zeros((8, 128), F32)
    weights.wait()

    @pl.loop(0, chunks)
    def _(block):
        at = pl.multiple_of(block * step, step)
        put_rows(senders, at, dot(halo[pl.ds(at, step), :], w_proc[0]))

    def pick(block, into):
        at = block * STEP
        pick_rows(lambda inner: pl.multiple_of(src[at + inner], 4), senders, into, 0, STEP, 4)

    def update(block, source):
        here = pl.ds(pl.multiple_of(block * STEP, STEP), STEP)
        hidden = silu(local[here, :].astype(F32) + get_rows(source, 0, STEP, 4)).astype(BF16)
        change = norm(dot(hidden, w_proc[1]), gains[2:3, :])
        new[here, :] = (edges[here, :].astype(F32) + change).astype(BF16)

    pick(0, first)

    @pl.loop(0, edge_chunks)
    def _(pair):
        edge_copy(pair).wait()
        local_copy(pair).wait()
        pick(pair * 2 + 1, second)
        update(pair * 2, first)
        pick(jnp.minimum(pair * 2 + 2, last), first)
        update(pair * 2 + 1, second)
        new_copy(pair).start()

    for part in range(edge_chunks):
        new_copy(part).wait()


def shards(
    grid_in,
    embed_in,
    embed_out,
    mesh_latent,
    edge_latent,
    enc_w,
    node_w,
    proc_w,
    gains,
    g2m_src,
    g2m_dst,
    g2m_count,
    halo_rows,
    proc_dst,
    proc_src,
):
    axes = ("band", "tile")
    peers = lax.axis_size("band") * lax.axis_size("tile")
    grid_rows, features = grid_in.shape
    mesh_rows, width = mesh_latent.shape
    edges = edge_latent.shape[0]
    cap = g2m_src.shape[2]
    halo_cap = halo_rows.shape[2]
    slots = peers * cap
    halo_slots = peers * halo_cap
    parts = width // 128

    def full(rows, columns, dtype):
        return jax.ShapeDtypeStruct((rows, columns), dtype)

    def scratch(rows, columns=128, dtype=F32):
        return pltpu.VMEM((rows, columns), dtype)

    def cost(flops, moved):
        return pl.CostEstimate(flops=flops, bytes_accessed=moved, transcendentals=0)

    def sems(*counts):
        return pltpu.SemaphoreType.DMA(counts)

    outgoing = pl.pallas_call(
        pick_grid,
        out_shape=full(slots, features, BF16),
        in_specs=[ANY, ANY],
        out_specs=VMEM,
        scratch_shapes=[
            pltpu.SMEM((cap, peers), jnp.int32),
            scratch(features, grid_rows, BF16),
            scratch(grid_rows * 2),
            scratch(slots * 2),
            scratch(256, STEP, BF16),
            pltpu.SemaphoreType.DMA,
            sems(grid_rows // (STEP * 2)),
        ],
        compiler_params=params(14),
        name="pick_grid",
    )(in_hbm(g2m_src[0].T), in_hbm(grid_in.T))
    arrived = lax.all_to_all(
        outgoing.reshape(peers, cap, features), axes, split_axis=0, concat_axis=0, tiled=True
    ).reshape(slots, features)

    dst = g2m_dst[0].T
    halo = halo_rows[0].T
    mesh_term, own, own_halo, folded = pl.pallas_call(
        mesh_side,
        out_shape=(
            pltpu.HBM((slots, width), BF16),
            pltpu.HBM((mesh_rows * parts, 128), F32),
            pltpu.HBM((halo_slots, width), BF16),
            full(width, width, BF16),
        ),
        in_specs=[SMEM, SMEM, ANY, ANY, ANY],
        out_specs=(ANY, ANY, ANY, VMEM),
        scratch_shapes=[
            scratch(mesh_rows * parts),
            scratch(mesh_rows * parts),
            scratch(halo_slots * parts),
            scratch(slots * parts),
            scratch(mesh_rows * parts),
            scratch(slots, width, BF16),
            scratch(halo_slots, width, BF16),
            scratch(mesh_rows, width, BF16),
            pltpu.VMEM((2, width, width), BF16),
            pltpu.VMEM((2, width, width), BF16),
            sems(2 + mesh_rows // 512),
        ],
        compiler_params=params(40),
        cost_estimate=cost(10**10, 2 * 10**7),
        name="mesh_side",
    )(dst, halo, in_hbm(mesh_latent), in_hbm(enc_w), in_hbm(node_w))

    live = jnp.arange(cap, dtype=jnp.int32)[:, None] < g2m_count
    sums, halo_out = pl.pallas_call(
        encode,
        out_shape=(
            pltpu.HBM((mesh_rows * parts, 128), F32),
            pltpu.HBM((halo_slots, width), BF16),
        ),
        in_specs=[SMEM, SMEM, VMEM, ANY, ANY, ANY, VMEM, VMEM, ANY, ANY, ANY, VMEM],
        out_specs=(ANY, ANY),
        scratch_shapes=[
            scratch(mesh_rows * parts + 8),
            scratch(slots, width, BF16),
            scratch(STEP * parts),
            scratch(STEP * parts),
            scratch(halo_slots, width, BF16),
            scratch(width, width, BF16),
            scratch(width, width, BF16),
            scratch(width, width, BF16),
            scratch(halo_slots, width, BF16),
            sems(6 + halo_slots // STEP // 2),
        ],
        compiler_params=params(24),
        name="encode",
    )(
        jnp.where(live, dst, mesh_rows), halo, arrived, in_hbm(mesh_term), in_hbm(own),
        in_hbm(own_halo), embed_in, embed_out, in_hbm(enc_w), folded, in_hbm(node_w), gains,
    )
    halo_in = lax.all_to_all(
        halo_out.reshape(peers, halo_cap, width), axes, split_axis=0, concat_axis=0, tiled=True
    ).reshape(halo_slots, width)

    remote = proc_src >= mesh_rows
    mesh_new, local = pl.pallas_call(
        local_terms,
        out_shape=(pltpu.HBM((mesh_rows, width), BF16), pltpu.HBM((edges, width), BF16)),
        in_specs=[SMEM, SMEM, ANY, ANY, ANY, ANY, VMEM, ANY],
        out_specs=(ANY, ANY),
        scratch_shapes=[
            scratch(mesh_rows * parts),
            scratch(mesh_rows, width, BF16),
            scratch(edges, width, BF16),
            scratch(mesh_rows, width, BF16),
            scratch(edges, width, BF16),
            scratch(width, width, BF16),
            pltpu.VMEM((3, width, width), BF16),
            scratch(mesh_rows * parts),
            scratch(mesh_rows * parts + 8),
            scratch(512 * parts),
            sems(2 + 2 * (mesh_rows // 512)),
            sems(2, edges // 512),
        ],
        compiler_params=params(40),
        cost_estimate=cost(2 * 10**10, 4 * 10**7),
        name="local_terms",
    )(
        proc_dst * parts,
        jnp.where(remote, mesh_rows, proc_src) * parts,
        in_hbm(sums),
        in_hbm(mesh_latent),
        in_hbm(node_w),
        in_hbm(proc_w),
        gains,
        in_hbm(edge_latent),
    )
    edge_new = pl.pallas_call(
        edge_update,
        out_shape=pltpu.HBM((edges, width), BF16),
        in_specs=[SMEM, VMEM, ANY, ANY, ANY, VMEM],
        out_specs=ANY,
        scratch_shapes=[
            pltpu.VMEM((2, width, width), BF16),
            scratch(edges, width, BF16),
            scratch(edges, width, BF16),
            scratch(edges, width, BF16),
            scratch(halo_slots * parts + 8),
            scratch(STEP * parts),
            scratch(STEP * parts),
            sems(1),
            sems(2, edges // 512),
        ],
        compiler_params=params(28),
        name="edge_update",
    )(
        jnp.where(remote, proc_src - mesh_rows, halo_slots) * parts,
        halo_in,
        in_hbm(proc_w),
        in_hbm(edge_latent),
        in_hbm(local),
        gains,
    )
    return (mesh_new, edge_new)


def solution(mesh):
    rows = P(("band", "tile"), None)
    slots = P(("band", "tile"), None, None)
    flat = P(("band", "tile"))
    in_specs = (
        rows, P(), P(), rows, rows, P(), P(), P(), P(), slots, slots, rows, slots, flat, flat,
    )
    return jax.shard_map(
        shards, mesh=mesh, in_specs=in_specs, out_specs=(rows, rows), check_vma=False
    )
```

```python
import jax
import jax.numpy as jnp
from jax import lax
from jax.experimental import pallas as pl
from jax.experimental.pallas import tpu as pltpu
from jax.sharding import PartitionSpec as P

F32 = jnp.float32
BF16 = jnp.bfloat16
VMEM = pl.BlockSpec(memory_space=pltpu.VMEM)
SMEM = pl.BlockSpec(memory_space=pltpu.SMEM)
ANY = pl.BlockSpec(memory_space=pl.ANY)
STEP = 256
MESSAGE_STEP = 1024
HALO_STEP = 512
EDGE_STEP = 512


def params(mebibytes):
    return pltpu.CompilerParams(vmem_limit_bytes=mebibytes * 2**20)


def in_hbm(array):
    return pltpu.with_memory_space_constraint(array, pltpu.HBM)


def dot(a, b):
    return jnp.dot(a, b, preferred_element_type=F32)


def silu(v):
    half = 0.5 * v
    return half + half * jnp.tanh(half)


def norm(value, gain):
    mean = jnp.mean(value, axis=-1, keepdims=True)
    centred = value - mean
    variance = jnp.mean(centred * centred, axis=-1, keepdims=True)
    return centred * lax.rsqrt(variance + 1e-05) * gain


def put_rows(table, start, value):
    rows, width = value.shape
    parts = width // 128
    for part in range(parts):
        table[pl.ds(start * parts + part, rows, stride=parts), :] = value[
            :, part * 128 : part * 128 + 128
        ]


def get_rows(table, start, rows, parts):
    return jnp.concatenate(
        [table[pl.ds(start * parts + part, rows, stride=parts), :] for part in range(parts)],
        axis=1,
    )


def slot_index(index, peer, inner, scale):
    cap = index.shape[0]
    return pl.multiple_of(index[inner % cap, peer + inner // cap] * scale, scale)


def pick_rows(at, table, target, base, rows, parts):
    for inner in range(rows):
        target[pl.ds(base * parts + inner * parts, parts), :] = table[pl.ds(at(inner), parts), :]


def pick_grid(
    index_in, grid_in, out_hbm, index, grid, table, picked, turned, out, index_sem, sems, out_sems
):
    features, rows = grid.shape
    slots = out.shape[0]
    step = STEP * 2

    def grid_copy(part):
        columns = pl.ds(pl.multiple_of(part * step, step), step)
        return pltpu.make_async_copy(grid_in.at[:, columns], grid.at[:, columns], sems.at[part])

    for part in range(rows // step):
        grid_copy(part).start()
    index_copy = pltpu.make_async_copy(index_in, index, index_sem)
    index_copy.start()

    @pl.loop(0, rows // STEP)
    def _(block):
        @pl.when(block % 2 == 0)
        def _():
            grid_copy(block // 2).wait()

        at = pl.multiple_of(block * STEP, STEP)
        turned[pl.ds(0, features), :] = grid[:, pl.ds(at, STEP)]
        put_rows(table, at, turned[...].T.astype(F32))

    index_copy.wait()
    step = 128
    span = slots // out_sems.shape[0]

    def out_copy(part):
        return pltpu.make_async_copy(
            piece(out, part, span), piece(out_hbm, part, span), out_sems.at[part]
        )

    for part in range(slots // span):

        @pl.loop(part * span // step, (part + 1) * span // step)
        def _(block):
            at = pl.multiple_of(block * step, step)
            first = block * (step // index.shape[0])
            pick_rows(lambda inner: slot_index(index, first, inner, 2), table, picked, at, step, 2)
            out[pl.ds(at, step), :] = get_rows(picked, at, step, 2)[:, :features].astype(BF16)

        out_copy(part).start()

    for part in range(slots // span):
        out_copy(part).wait()


def piece(ref, part, rows):
    return ref.at[pl.ds(pl.multiple_of(part * rows, rows), rows)]


def mesh_side(
    dst, halo, mesh, enc_w, node_w,
    term_out, own_out, halo_out, folded_out,
    table, copies, picked, picked_too, own, terms, halves, latents, w_enc, w_node, sems,
):
    rows = mesh.shape[0]
    slots = halo_out.shape[0]
    step = 512
    chunks = rows // step
    weights = [
        pltpu.make_async_copy(enc_w.at[pl.ds(1, 2)], w_enc, sems.at[0]),
        pltpu.make_async_copy(node_w.at[pl.ds(0, 2)], w_node, sems.at[1]),
    ]
    for copy in weights:
        copy.start()

    def latent_copy(part):
        return pltpu.make_async_copy(
            piece(mesh, part, step), piece(latents, part, step), sems.at[2 + part]
        )

    for part in range(chunks):
        latent_copy(part).start()
    for copy in weights:
        copy.wait()

    @pl.loop(0, chunks)
    def _(block):
        at = pl.multiple_of(block * step, step)
        latent_copy(block).wait()
        value = latents[pl.ds(at, step), :]
        put_rows(table, at, dot(value, w_enc[0]))
        put_rows(own, at, dot(value, w_node[0]))
        put_rows(copies, at, value.astype(F32))

    outs = [pltpu.make_async_copy(own, own_out, sems.at[0])]
    outs[0].start()
    folded_out[...] = dot(w_enc[1], w_node[1]).astype(BF16)
    step = 64
    parts = 4
    span = slots // parts
    for part in range(parts):

        @pl.loop(part * span // step, (part + 1) * span // step)
        def _(block):
            at = pl.multiple_of(block * step, step)
            pick_rows(lambda inner: slot_index(dst, block * (step // dst.shape[0]), inner, 4), table, picked_too, at, step, 4)
            pick_rows(lambda inner: slot_index(halo, block * (step // halo.shape[0]), inner, 4), copies, picked, at, step, 4)
            terms[pl.ds(at, step), :] = get_rows(picked_too, at, step, 4).astype(BF16)
            halves[pl.ds(at, step), :] = get_rows(picked, at, step, 4).astype(BF16)

        outs.append(
            pltpu.make_async_copy(
                piece(terms, part, span), piece(term_out, part, span), sems.at[2 + part]
            )
        )
        outs[-1].start()
    outs.append(pltpu.make_async_copy(halves, halo_out, sems.at[1]))
    outs[-1].start()
    for copy in outs:
        copy.wait()


def node_update(pre, own, w_out, gain):
    return (own.astype(F32) + norm(dot(silu(pre).astype(BF16), w_out), gain)).astype(BF16)


def encode(
    target, halo, rows_in, mesh_term, own, own_halo, embed_in, embed_out, enc_w, folded, node_w,
    gains, sums_out, halo_out,
    sums, terms, sent, first, second, halves, w_grid, w_message, w_out, halo_rows, sems,
):
    slots = rows_in.shape[0]
    mesh_rows = own.shape[0]
    blocks = slots // HALO_STEP
    copies = [
        pltpu.make_async_copy(enc_w.at[0], w_grid, sems.at[0]),
        pltpu.make_async_copy(folded, w_message, sems.at[1]),
        pltpu.make_async_copy(mesh_term, terms, sems.at[2]),
        pltpu.make_async_copy(own, sums.at[pl.ds(0, mesh_rows)], sems.at[3]),
        pltpu.make_async_copy(node_w.at[2], w_out, sems.at[4]),
        pltpu.make_async_copy(own_halo, halves, sems.at[5]),
    ]
    for copy in copies:
        copy.start()
    sums[pl.ds(mesh_rows, 8), :] = jnp.zeros((8, 128), F32)
    for copy in copies[:3]:
        copy.wait()
    step = MESSAGE_STEP

    @pl.loop(0, slots // step)
    def _(block):
        at = pl.multiple_of(block * step, step)
        hidden = silu(dot(rows_in[pl.ds(at, step), :], embed_in[...])).astype(BF16)
        latent = norm(dot(hidden, embed_out[...]), gains[0:1, :]).astype(BF16)
        pre = dot(latent, w_grid[...]) + terms[pl.ds(at, step), :].astype(F32)
        put_rows(sent, at, dot(silu(pre).astype(BF16), w_message[...]))

    copies[3].wait()

    @pl.loop(0, slots // 32)
    def _(block):
        for inner in range(32):
            row = block * 32 + inner
            to = pl.ds(pl.multiple_of(target[row], 4), 4)
            sums[to, :] = sums[to, :] + sent[pl.ds(pl.multiple_of(row * 4, 4), 4), :]

    sums_copy = pltpu.make_async_copy(sums.at[pl.ds(0, mesh_rows)], sums_out, sems.at[3])
    sums_copy.start()
    for copy in copies[4:]:
        copy.wait()

    def pick(block, into):
        at = block * HALO_STEP
        pick_rows(
            lambda inner: pl.multiple_of(halo[at + inner], 4), sums, into, 0, HALO_STEP, 4
        )

    def update(block, source):
        at = pl.multiple_of(block * HALO_STEP, HALO_STEP)
        halo_rows[pl.ds(at, HALO_STEP), :] = node_update(
            get_rows(source, 0, HALO_STEP, 4), halves[pl.ds(at, HALO_STEP), :], w_out[...], gains[1:2, :]
        )

    pick(0, first)

    def halo_copy(pair):
        return pltpu.make_async_copy(
            piece(halo_rows, pair, HALO_STEP * 2), piece(halo_out, pair, HALO_STEP * 2), sems.at[6 + pair]
        )

    @pl.loop(0, blocks // 2)
    def _(pair):
        pick(pair * 2 + 1, second)
        update(pair * 2, first)
        pick(jnp.minimum(pair * 2 + 2, blocks - 1), first)
        update(pair * 2 + 1, second)
        halo_copy(pair).start()

    sums_copy.wait()
    for pair in range(blocks // 2):
        halo_copy(pair).wait()


def local_terms(
    dst, src, sums_in, mesh, node_w, proc_w, gains, edges_in, mesh_out, out,
    sums, latents, edges, new, local, w_node, w_proc, receivers, senders, picked, sems, edge_sems,
):
    rows = mesh.shape[0]
    step = 512
    chunks = rows // step
    edge_chunks = edges.shape[0] // step
    weights = [
        pltpu.make_async_copy(node_w.at[2], w_node, sems.at[0]),
        pltpu.make_async_copy(proc_w.at[pl.ds(0, 3)], w_proc, sems.at[1]),
    ]

    def sums_copy(part):
        return pltpu.make_async_copy(
            piece(sums_in, part, step * 4), piece(sums, part, step * 4), sems.at[2 + part]
        )

    def latent_copy(part):
        return pltpu.make_async_copy(
            piece(mesh, part, step), piece(latents, part, step), sems.at[2 + chunks + part]
        )

    def new_copy(part):
        return pltpu.make_async_copy(
            piece(new, part, step), piece(mesh_out, part, step), sems.at[2 + part]
        )

    def edge_copy(part):
        return pltpu.make_async_copy(
            piece(edges_in, part, step), piece(edges, part, step), edge_sems.at[0, part]
        )

    def local_copy(part):
        return pltpu.make_async_copy(
            piece(local, part, step), piece(out, part, step), edge_sems.at[1, part]
        )

    for copy in weights:
        copy.start()
    for part in range(chunks):
        sums_copy(part).start()
        latent_copy(part).start()
    for part in range(edge_chunks):
        edge_copy(part).start()
    senders[pl.ds(rows * 4, 8), :] = jnp.zeros((8, 128), F32)
    for copy in weights:
        copy.wait()

    @pl.loop(0, chunks)
    def _(block):
        at = pl.multiple_of(block * step, step)
        sums_copy(block).wait()
        latent_copy(block).wait()
        value = node_update(
            get_rows(sums, at, step, 4), latents[pl.ds(at, step), :], w_node[...], gains[1:2, :]
        )
        new[pl.ds(at, step), :] = value
        put_rows(receivers, at, dot(value, w_proc[1]))
        put_rows(senders, at, dot(value, w_proc[2]))
        new_copy(block).start()

    @pl.loop(0, edge_chunks)
    def _(block):
        start = pl.multiple_of(block * step, step)
        edge_copy(block).wait()

        @pl.loop(0, step // 32)
        def _(group):
            for inner in range(32):
                row = group * 32 + inner
                one = pl.multiple_of(dst[start + row], 4)
                two = pl.multiple_of(src[start + row], 4)
                picked[pl.ds(pl.multiple_of(row * 4, 4), 4), :] = (
                    receivers[pl.ds(one, 4), :] + senders[pl.ds(two, 4), :]
                )

        here = pl.ds(start, step)
        value = dot(edges[here, :], w_proc[0]) + get_rows(picked, 0, step, 4)
        local[here, :] = value.astype(BF16)
        local_copy(block).start()

    for part in range(chunks):
        new_copy(part).wait()
    for part in range(edge_chunks):
        local_copy(part).wait()


def edge_update(
    src, halo, proc_w, edges_in, local_in, gains, out,
    w_proc, edges, local, new, senders, first, second, sems, edge_sems,
):
    rows = halo.shape[0]
    step = 512
    chunks = rows // step
    edge_step = EDGE_STEP * 2
    edge_chunks = edges.shape[0] // edge_step
    last = src.shape[0] // EDGE_STEP - 1
    weights = pltpu.make_async_copy(proc_w.at[pl.ds(2, 2)], w_proc, sems.at[0])

    def edge_copy(part):
        return pltpu.make_async_copy(
            piece(edges_in, part, edge_step), piece(edges, part, edge_step), edge_sems.at[0, part]
        )

    def local_copy(part):
        return pltpu.make_async_copy(
            piece(local_in, part, edge_step), piece(local, part, edge_step), edge_sems.at[1, part]
        )

    def new_copy(part):
        return pltpu.make_async_copy(
            piece(new, part, edge_step), piece(out, part, edge_step), edge_sems.at[0, part]
        )

    weights.start()
    for part in range(edge_chunks):
        local_copy(part).start()
        edge_copy(part).start()
    senders[pl.ds(rows * 4, 8), :] = jnp.zeros((8, 128), F32)
    weights.wait()

    @pl.loop(0, chunks)
    def _(block):
        at = pl.multiple_of(block * step, step)
        put_rows(senders, at, dot(halo[pl.ds(at, step), :], w_proc[0]))

    def pick(block, into):
        at = block * EDGE_STEP
        pick_rows(lambda inner: pl.multiple_of(src[at + inner], 4), senders, into, 0, EDGE_STEP, 4)

    def update(block, source):
        here = pl.ds(pl.multiple_of(block * EDGE_STEP, EDGE_STEP), EDGE_STEP)
        hidden = silu(local[here, :].astype(F32) + get_rows(source, 0, EDGE_STEP, 4)).astype(BF16)
        change = norm(dot(hidden, w_proc[1]), gains[2:3, :])
        new[here, :] = (edges[here, :].astype(F32) + change).astype(BF16)

    pick(0, first)

    @pl.loop(0, edge_chunks)
    def _(pair):
        edge_copy(pair).wait()
        local_copy(pair).wait()
        pick(pair * 2 + 1, second)
        update(pair * 2, first)
        pick(jnp.minimum(pair * 2 + 2, last), first)
        update(pair * 2 + 1, second)
        new_copy(pair).start()

    for part in range(edge_chunks):
        new_copy(part).wait()


def shards(
    grid_in,
    embed_in,
    embed_out,
    mesh_latent,
    edge_latent,
    enc_w,
    node_w,
    proc_w,
    gains,
    g2m_src,
    g2m_dst,
    g2m_count,
    halo_rows,
    proc_dst,
    proc_src,
):
    axes = ("band", "tile")
    peers = lax.axis_size("band") * lax.axis_size("tile")
    grid_rows, features = grid_in.shape
    mesh_rows, width = mesh_latent.shape
    edges = edge_latent.shape[0]
    cap = g2m_src.shape[2]
    halo_cap = halo_rows.shape[2]
    slots = peers * cap
    halo_slots = peers * halo_cap
    parts = width // 128

    def full(rows, columns, dtype):
        return jax.ShapeDtypeStruct((rows, columns), dtype)

    def scratch(rows, columns=128, dtype=F32):
        return pltpu.VMEM((rows, columns), dtype)

    def cost(flops, moved):
        return pl.CostEstimate(flops=flops, bytes_accessed=moved, transcendentals=0)

    def sems(*counts):
        return pltpu.SemaphoreType.DMA(counts)

    outgoing = pl.pallas_call(
        pick_grid,
        out_shape=pltpu.HBM((slots, features), BF16),
        in_specs=[ANY, ANY],
        out_specs=ANY,
        scratch_shapes=[
            pltpu.SMEM((cap, peers), jnp.int32),
            scratch(features, grid_rows, BF16),
            scratch(grid_rows * 2),
            scratch(slots * 2),
            scratch(256, STEP, BF16),
            scratch(slots, features, BF16),
            pltpu.SemaphoreType.DMA,
            sems(grid_rows // (STEP * 2)),
            sems(4),
        ],
        compiler_params=params(14),
        name="pick_grid",
    )(in_hbm(g2m_src[0].T), in_hbm(grid_in.T))
    arrived = lax.all_to_all(
        outgoing.reshape(peers, cap, features), axes, split_axis=0, concat_axis=0, tiled=True
    ).reshape(slots, features)

    dst = g2m_dst[0].T
    halo = halo_rows[0].T
    mesh_term, own, own_halo, folded = pl.pallas_call(
        mesh_side,
        out_shape=(
            pltpu.HBM((slots, width), BF16),
            pltpu.HBM((mesh_rows * parts, 128), F32),
            pltpu.HBM((halo_slots, width), BF16),
            full(width, width, BF16),
        ),
        in_specs=[SMEM, SMEM, ANY, ANY, ANY],
        out_specs=(ANY, ANY, ANY, VMEM),
        scratch_shapes=[
            scratch(mesh_rows * parts),
            scratch(mesh_rows * parts),
            scratch(halo_slots * parts),
            scratch(slots * parts),
            scratch(mesh_rows * parts),
            scratch(slots, width, BF16),
            scratch(halo_slots, width, BF16),
            scratch(mesh_rows, width, BF16),
            pltpu.VMEM((2, width, width), BF16),
            pltpu.VMEM((2, width, width), BF16),
            sems(2 + mesh_rows // 512),
        ],
        compiler_params=params(40),
        cost_estimate=cost(10**10, 2 * 10**7),
        name="mesh_side",
    )(dst, halo, in_hbm(mesh_latent), in_hbm(enc_w), in_hbm(node_w))

    live = jnp.arange(cap, dtype=jnp.int32)[:, None] < g2m_count
    sums, halo_out = pl.pallas_call(
        encode,
        out_shape=(
            pltpu.HBM((mesh_rows * parts, 128), F32),
            pltpu.HBM((halo_slots, width), BF16),
        ),
        in_specs=[SMEM, SMEM, VMEM, ANY, ANY, ANY, VMEM, VMEM, ANY, ANY, ANY, VMEM],
        out_specs=(ANY, ANY),
        scratch_shapes=[
            scratch(mesh_rows * parts + 8),
            scratch(slots, width, BF16),
            scratch(slots * parts),
            scratch(HALO_STEP * parts),
            scratch(HALO_STEP * parts),
            scratch(halo_slots, width, BF16),
            scratch(width, width, BF16),
            scratch(width, width, BF16),
            scratch(width, width, BF16),
            scratch(halo_slots, width, BF16),
            sems(6 + halo_slots // HALO_STEP // 2),
        ],
        compiler_params=params(32),
        name="encode",
    )(
        jnp.where(live, dst, mesh_rows).T.reshape(-1) * parts, halo.T.reshape(-1) * parts, arrived, in_hbm(mesh_term), in_hbm(own),
        in_hbm(own_halo), embed_in, embed_out, in_hbm(enc_w), folded, in_hbm(node_w), gains,
    )
    halo_in = lax.all_to_all(
        halo_out.reshape(peers, halo_cap, width), axes, split_axis=0, concat_axis=0, tiled=True
    ).reshape(halo_slots, width)

    remote = proc_src >= mesh_rows
    mesh_new, local = pl.pallas_call(
        local_terms,
        out_shape=(pltpu.HBM((mesh_rows, width), BF16), pltpu.HBM((edges, width), BF16)),
        in_specs=[SMEM, SMEM, ANY, ANY, ANY, ANY, VMEM, ANY],
        out_specs=(ANY, ANY),
        scratch_shapes=[
            scratch(mesh_rows * parts),
            scratch(mesh_rows, width, BF16),
            scratch(edges, width, BF16),
            scratch(mesh_rows, width, BF16),
            scratch(edges, width, BF16),
            scratch(width, width, BF16),
            pltpu.VMEM((3, width, width), BF16),
            scratch(mesh_rows * parts),
            scratch(mesh_rows * parts + 8),
            scratch(512 * parts),
            sems(2 + 2 * (mesh_rows // 512)),
            sems(2, edges // 512),
        ],
        compiler_params=params(40),
        cost_estimate=cost(2 * 10**10, 4 * 10**7),
        name="local_terms",
    )(
        proc_dst * parts,
        jnp.where(remote, mesh_rows, proc_src) * parts,
        in_hbm(sums),
        in_hbm(mesh_latent),
        in_hbm(node_w),
        in_hbm(proc_w),
        gains,
        in_hbm(edge_latent),
    )
    edge_new = pl.pallas_call(
        edge_update,
        out_shape=pltpu.HBM((edges, width), BF16),
        in_specs=[SMEM, VMEM, ANY, ANY, ANY, VMEM],
        out_specs=ANY,
        scratch_shapes=[
            pltpu.VMEM((2, width, width), BF16),
            scratch(edges, width, BF16),
            scratch(edges, width, BF16),
            scratch(edges, width, BF16),
            scratch(halo_slots * parts + 8),
            scratch(EDGE_STEP * parts),
            scratch(EDGE_STEP * parts),
            sems(1),
            sems(2, edges // EDGE_STEP // 2),
        ],
        compiler_params=params(28),
        name="edge_update",
    )(
        jnp.where(remote, proc_src - mesh_rows, halo_slots) * parts,
        halo_in,
        in_hbm(proc_w),
        in_hbm(edge_latent),
        in_hbm(local),
        gains,
    )
    return (mesh_new, edge_new)


def solution(mesh):
    rows = P(("band", "tile"), None)
    slots = P(("band", "tile"), None, None)
    flat = P(("band", "tile"))
    in_specs = (
        rows, P(), P(), rows, rows, P(), P(), P(), P(), slots, slots, rows, slots, flat, flat,
    )
    return jax.shard_map(
        shards, mesh=mesh, in_specs=in_specs, out_specs=(rows, rows), check_vma=False
    )
```

```python
import jax
import jax.numpy as jnp
from jax import lax
from jax.experimental import pallas as pl
from jax.experimental.pallas import tpu as pltpu
from jax.sharding import PartitionSpec as P

F32 = jnp.float32
BF16 = jnp.bfloat16
VMEM = pl.BlockSpec(memory_space=pltpu.VMEM)
SMEM = pl.BlockSpec(memory_space=pltpu.SMEM)
ANY = pl.BlockSpec(memory_space=pl.ANY)
STEP = 256
MESSAGE_STEP = 1024
HALO_STEP = 512
EDGE_STEP = 512


def params(mebibytes):
    return pltpu.CompilerParams(vmem_limit_bytes=mebibytes * 2**20)


def in_hbm(array):
    return pltpu.with_memory_space_constraint(array, pltpu.HBM)


def dot(a, b):
    return jnp.dot(a, b, preferred_element_type=F32)


def silu(v):
    half = 0.5 * v
    return half + half * jnp.tanh(half)


def norm(value, gain):
    mean = jnp.mean(value, axis=-1, keepdims=True)
    centred = value - mean
    variance = jnp.mean(centred * centred, axis=-1, keepdims=True)
    return centred * lax.rsqrt(variance + 1e-05) * gain


def put_rows(table, start, value):
    rows, width = value.shape
    parts = width // 128
    for part in range(parts):
        table[pl.ds(start * parts + part, rows, stride=parts), :] = value[
            :, part * 128 : part * 128 + 128
        ]


def get_rows(table, start, rows, parts):
    return jnp.concatenate(
        [table[pl.ds(start * parts + part, rows, stride=parts), :] for part in range(parts)],
        axis=1,
    )


def slot_index(index, peer, inner, scale):
    cap = index.shape[0]
    return pl.multiple_of(index[inner % cap, peer + inner // cap] * scale, scale)


def pick_rows(at, table, target, base, rows, parts):
    for inner in range(rows):
        target[pl.ds(base * parts + inner * parts, parts), :] = table[pl.ds(at(inner), parts), :]


def pick_grid(
    index_in, grid_in, out_hbm, index, grid, table, picked, turned, out, index_sem, sems, out_sems
):
    features, rows = grid.shape
    slots = out.shape[0]
    step = STEP * 2

    def grid_copy(part):
        columns = pl.ds(pl.multiple_of(part * step, step), step)
        return pltpu.make_async_copy(grid_in.at[:, columns], grid.at[:, columns], sems.at[part])

    for part in range(rows // step):
        grid_copy(part).start()
    index_copy = pltpu.make_async_copy(index_in, index, index_sem)
    index_copy.start()

    @pl.loop(0, rows // STEP)
    def _(block):
        @pl.when(block % 2 == 0)
        def _():
            grid_copy(block // 2).wait()

        at = pl.multiple_of(block * STEP, STEP)
        turned[pl.ds(0, features), :] = grid[:, pl.ds(at, STEP)]
        put_rows(table, at, turned[...].T.astype(F32))

    index_copy.wait()
    step = 128
    span = slots // out_sems.shape[0]

    def out_copy(part):
        return pltpu.make_async_copy(
            piece(out, part, span), piece(out_hbm, part, span), out_sems.at[part]
        )

    for part in range(slots // span):

        @pl.loop(part * span // step, (part + 1) * span // step)
        def _(block):
            at = pl.multiple_of(block * step, step)
            first = block * (step // index.shape[0])
            pick_rows(lambda inner: slot_index(index, first, inner, 2), table, picked, at, step, 2)
            out[pl.ds(at, step), :] = get_rows(picked, at, step, 2)[:, :features].astype(BF16)

        out_copy(part).start()

    for part in range(slots // span):
        out_copy(part).wait()


def piece(ref, part, rows):
    return ref.at[pl.ds(pl.multiple_of(part * rows, rows), rows)]


def mesh_side(
    dst, halo, mesh, enc_w, node_w,
    term_out, own_out, halo_out, folded_out,
    table, copies, picked, picked_too, own, terms, halves, latents, w_enc, w_node, sems,
):
    rows = mesh.shape[0]
    slots = halo_out.shape[0]
    step = 512
    chunks = rows // step
    weights = [
        pltpu.make_async_copy(enc_w.at[pl.ds(1, 2)], w_enc, sems.at[0]),
        pltpu.make_async_copy(node_w.at[pl.ds(0, 2)], w_node, sems.at[1]),
    ]
    for copy in weights:
        copy.start()

    def latent_copy(part):
        return pltpu.make_async_copy(
            piece(mesh, part, step), piece(latents, part, step), sems.at[2 + part]
        )

    for part in range(chunks):
        latent_copy(part).start()
    for copy in weights:
        copy.wait()

    @pl.loop(0, chunks)
    def _(block):
        at = pl.multiple_of(block * step, step)
        latent_copy(block).wait()
        value = latents[pl.ds(at, step), :]
        put_rows(table, at, dot(value, w_enc[0]))
        put_rows(own, at, dot(value, w_node[0]))
        put_rows(copies, at, value.astype(F32))

    outs = [pltpu.make_async_copy(own, own_out, sems.at[0])]
    outs[0].start()
    folded_out[...] = dot(w_enc[1], w_node[1]).astype(BF16)
    step = 64
    parts = 4
    span = slots // parts
    for part in range(parts):

        @pl.loop(part * span // step, (part + 1) * span // step)
        def _(block):
            at = pl.multiple_of(block * step, step)
            pick_rows(lambda inner: slot_index(dst, block * (step // dst.shape[0]), inner, 4), table, picked_too, at, step, 4)
            pick_rows(lambda inner: slot_index(halo, block * (step // halo.shape[0]), inner, 4), copies, picked, at, step, 4)
            terms[pl.ds(at, step), :] = get_rows(picked_too, at, step, 4).astype(BF16)
            halves[pl.ds(at, step), :] = get_rows(picked, at, step, 4).astype(BF16)

        outs.append(
            pltpu.make_async_copy(
                piece(terms, part, span), piece(term_out, part, span), sems.at[2 + part]
            )
        )
        outs[-1].start()
    outs.append(pltpu.make_async_copy(halves, halo_out, sems.at[1]))
    outs[-1].start()
    for copy in outs:
        copy.wait()


def node_update(pre, own, w_out, gain):
    return (own.astype(F32) + norm(dot(silu(pre).astype(BF16), w_out), gain)).astype(BF16)


def encode(
    target, halo, rows_in, mesh_term, own, own_halo, embed_in, embed_out, enc_w, folded, node_w,
    gains, sums_out, halo_out,
    sums, terms, sent, first, second, halves, w_grid, w_message, w_out, halo_rows, sems,
):
    slots = rows_in.shape[0]
    mesh_rows = own.shape[0]
    blocks = slots // HALO_STEP
    copies = [
        pltpu.make_async_copy(enc_w.at[0], w_grid, sems.at[0]),
        pltpu.make_async_copy(folded, w_message, sems.at[1]),
        pltpu.make_async_copy(mesh_term, terms, sems.at[2]),
        pltpu.make_async_copy(own, sums.at[pl.ds(0, mesh_rows)], sems.at[3]),
        pltpu.make_async_copy(node_w.at[2], w_out, sems.at[4]),
        pltpu.make_async_copy(own_halo, halves, sems.at[5]),
    ]
    for copy in copies:
        copy.start()
    spare = sums.shape[0] - mesh_rows
    sums[pl.ds(mesh_rows, spare), :] = jnp.zeros((spare, 128), F32)
    for copy in copies[:3]:
        copy.wait()
    step = MESSAGE_STEP

    @pl.loop(0, slots // step)
    def _(block):
        at = pl.multiple_of(block * step, step)
        hidden = silu(dot(rows_in[pl.ds(at, step), :], embed_in[...])).astype(BF16)
        latent = norm(dot(hidden, embed_out[...]), gains[0:1, :]).astype(BF16)
        pre = dot(latent, w_grid[...]) + terms[pl.ds(at, step), :].astype(F32)
        put_rows(sent, at, dot(silu(pre).astype(BF16), w_message[...]))

    copies[3].wait()

    @pl.loop(0, slots // 32)
    def _(block):
        for inner in range(32):
            row = block * 32 + inner
            to = pl.ds(pl.multiple_of(target[row], 4), 4)
            sums[to, :] = sums[to, :] + sent[pl.ds(pl.multiple_of(row * 4, 4), 4), :]

    sums_copy = pltpu.make_async_copy(sums.at[pl.ds(0, mesh_rows)], sums_out, sems.at[3])
    sums_copy.start()
    for copy in copies[4:]:
        copy.wait()

    def pick(block, into):
        at = block * HALO_STEP
        pick_rows(
            lambda inner: pl.multiple_of(halo[at + inner], 4), sums, into, 0, HALO_STEP, 4
        )

    def update(block, source):
        at = pl.multiple_of(block * HALO_STEP, HALO_STEP)
        halo_rows[pl.ds(at, HALO_STEP), :] = node_update(
            get_rows(source, 0, HALO_STEP, 4), halves[pl.ds(at, HALO_STEP), :], w_out[...], gains[1:2, :]
        )

    pick(0, first)

    def halo_copy(pair):
        return pltpu.make_async_copy(
            piece(halo_rows, pair, HALO_STEP * 2), piece(halo_out, pair, HALO_STEP * 2), sems.at[6 + pair]
        )

    @pl.loop(0, blocks // 2)
    def _(pair):
        pick(pair * 2 + 1, second)
        update(pair * 2, first)
        pick(jnp.minimum(pair * 2 + 2, blocks - 1), first)
        update(pair * 2 + 1, second)
        halo_copy(pair).start()

    sums_copy.wait()
    for pair in range(blocks // 2):
        halo_copy(pair).wait()


def local_terms(
    dst, src, sums_in, mesh, node_w, proc_w, gains, edges_in, mesh_out, out,
    sums, latents, edges, new, local, w_node, w_proc, receivers, senders, picked, sems, edge_sems,
):
    rows = mesh.shape[0]
    step = 512
    chunks = rows // step
    edge_chunks = edges.shape[0] // step
    weights = [
        pltpu.make_async_copy(node_w.at[2], w_node, sems.at[0]),
        pltpu.make_async_copy(proc_w.at[pl.ds(0, 3)], w_proc, sems.at[1]),
    ]

    def sums_copy(part):
        return pltpu.make_async_copy(
            piece(sums_in, part, step * 4), piece(sums, part, step * 4), sems.at[2 + part]
        )

    def latent_copy(part):
        return pltpu.make_async_copy(
            piece(mesh, part, step), piece(latents, part, step), sems.at[2 + chunks + part]
        )

    def new_copy(part):
        return pltpu.make_async_copy(
            piece(new, part, step), piece(mesh_out, part, step), sems.at[2 + part]
        )

    def edge_copy(part):
        return pltpu.make_async_copy(
            piece(edges_in, part, step), piece(edges, part, step), edge_sems.at[0, part]
        )

    def local_copy(part):
        return pltpu.make_async_copy(
            piece(local, part, step), piece(out, part, step), edge_sems.at[1, part]
        )

    for copy in weights:
        copy.start()
    for part in range(chunks):
        sums_copy(part).start()
        latent_copy(part).start()
    for part in range(edge_chunks):
        edge_copy(part).start()
    senders[pl.ds(rows * 4, 8), :] = jnp.zeros((8, 128), F32)
    for copy in weights:
        copy.wait()

    @pl.loop(0, chunks)
    def _(block):
        at = pl.multiple_of(block * step, step)
        sums_copy(block).wait()
        latent_copy(block).wait()
        value = node_update(
            get_rows(sums, at, step, 4), latents[pl.ds(at, step), :], w_node[...], gains[1:2, :]
        )
        new[pl.ds(at, step), :] = value
        put_rows(receivers, at, dot(value, w_proc[1]))
        put_rows(senders, at, dot(value, w_proc[2]))
        new_copy(block).start()

    @pl.loop(0, edge_chunks)
    def _(block):
        start = pl.multiple_of(block * step, step)
        edge_copy(block).wait()

        @pl.loop(0, step // 32)
        def _(group):
            for inner in range(32):
                row = group * 32 + inner
                one = pl.multiple_of(dst[start + row], 4)
                two = pl.multiple_of(src[start + row], 4)
                picked[pl.ds(pl.multiple_of(row * 4, 4), 4), :] = (
                    receivers[pl.ds(one, 4), :] + senders[pl.ds(two, 4), :]
                )

        here = pl.ds(start, step)
        value = dot(edges[here, :], w_proc[0]) + get_rows(picked, 0, step, 4)
        local[here, :] = value.astype(BF16)
        local_copy(block).start()

    for part in range(chunks):
        new_copy(part).wait()
    for part in range(edge_chunks):
        local_copy(part).wait()


def edge_update(
    src, halo, proc_w, edges_in, local_in, gains, out,
    w_proc, edges, local, new, senders, first, second, sems, edge_sems,
):
    rows = halo.shape[0]
    step = 1024
    chunks = rows // step
    edge_step = EDGE_STEP * 2
    edge_chunks = edges.shape[0] // edge_step
    last = src.shape[0] // EDGE_STEP - 1
    weights = pltpu.make_async_copy(proc_w.at[pl.ds(2, 2)], w_proc, sems.at[0])

    def edge_copy(part):
        return pltpu.make_async_copy(
            piece(edges_in, part, edge_step), piece(edges, part, edge_step), edge_sems.at[0, part]
        )

    def local_copy(part):
        return pltpu.make_async_copy(
            piece(local_in, part, edge_step), piece(local, part, edge_step), edge_sems.at[1, part]
        )

    def new_copy(part):
        return pltpu.make_async_copy(
            piece(new, part, edge_step), piece(out, part, edge_step), edge_sems.at[0, part]
        )

    weights.start()
    for part in range(edge_chunks):
        local_copy(part).start()
        edge_copy(part).start()
    senders[pl.ds(rows * 4, 8), :] = jnp.zeros((8, 128), F32)
    weights.wait()

    @pl.loop(0, chunks)
    def _(block):
        at = pl.multiple_of(block * step, step)
        put_rows(senders, at, dot(halo[pl.ds(at, step), :], w_proc[0]))

    def pick(block, into):
        at = block * EDGE_STEP
        pick_rows(lambda inner: pl.multiple_of(src[at + inner], 4), senders, into, 0, EDGE_STEP, 4)

    def update(block, source):
        here = pl.ds(pl.multiple_of(block * EDGE_STEP, EDGE_STEP), EDGE_STEP)
        hidden = silu(local[here, :].astype(F32) + get_rows(source, 0, EDGE_STEP, 4)).astype(BF16)
        change = norm(dot(hidden, w_proc[1]), gains[2:3, :])
        new[here, :] = (edges[here, :].astype(F32) + change).astype(BF16)

    pick(0, first)

    @pl.loop(0, edge_chunks)
    def _(pair):
        edge_copy(pair).wait()
        local_copy(pair).wait()
        pick(pair * 2 + 1, second)
        update(pair * 2, first)
        pick(jnp.minimum(pair * 2 + 2, last), first)
        update(pair * 2 + 1, second)
        new_copy(pair).start()

    for part in range(edge_chunks):
        new_copy(part).wait()


def shards(
    grid_in,
    embed_in,
    embed_out,
    mesh_latent,
    edge_latent,
    enc_w,
    node_w,
    proc_w,
    gains,
    g2m_src,
    g2m_dst,
    g2m_count,
    halo_rows,
    proc_dst,
    proc_src,
):
    axes = ("band", "tile")
    peers = lax.axis_size("band") * lax.axis_size("tile")
    grid_rows, features = grid_in.shape
    mesh_rows, width = mesh_latent.shape
    edges = edge_latent.shape[0]
    cap = g2m_src.shape[2]
    halo_cap = halo_rows.shape[2]
    slots = peers * cap
    halo_slots = peers * halo_cap
    parts = width // 128

    def full(rows, columns, dtype):
        return jax.ShapeDtypeStruct((rows, columns), dtype)

    def scratch(rows, columns=128, dtype=F32):
        return pltpu.VMEM((rows, columns), dtype)

    def cost(flops, moved):
        return pl.CostEstimate(flops=flops, bytes_accessed=moved, transcendentals=0)

    def sems(*counts):
        return pltpu.SemaphoreType.DMA(counts)

    outgoing = pl.pallas_call(
        pick_grid,
        out_shape=pltpu.HBM((slots, features), BF16),
        in_specs=[ANY, ANY],
        out_specs=ANY,
        scratch_shapes=[
            pltpu.SMEM((cap, peers), jnp.int32),
            scratch(features, grid_rows, BF16),
            scratch(grid_rows * 2),
            scratch(slots * 2),
            scratch(256, STEP, BF16),
            scratch(slots, features, BF16),
            pltpu.SemaphoreType.DMA,
            sems(grid_rows // (STEP * 2)),
            sems(4),
        ],
        compiler_params=params(14),
        name="pick_grid",
    )(in_hbm(g2m_src[0].T), in_hbm(grid_in.T))
    arrived = lax.all_to_all(
        outgoing.reshape(peers, cap, features), axes, split_axis=0, concat_axis=0, tiled=True
    ).reshape(slots, features)

    dst = g2m_dst[0].T
    halo = halo_rows[0].T
    mesh_term, own, own_halo, folded = pl.pallas_call(
        mesh_side,
        out_shape=(
            pltpu.HBM((slots, width), BF16),
            pltpu.HBM((mesh_rows * parts, 128), F32),
            pltpu.HBM((halo_slots, width), BF16),
            full(width, width, BF16),
        ),
        in_specs=[SMEM, SMEM, ANY, ANY, ANY],
        out_specs=(ANY, ANY, ANY, VMEM),
        scratch_shapes=[
            scratch(mesh_rows * parts),
            scratch(mesh_rows * parts),
            scratch(halo_slots * parts),
            scratch(slots * parts),
            scratch(mesh_rows * parts),
            scratch(slots, width, BF16),
            scratch(halo_slots, width, BF16),
            scratch(mesh_rows, width, BF16),
            pltpu.VMEM((2, width, width), BF16),
            pltpu.VMEM((2, width, width), BF16),
            sems(2 + mesh_rows // 512),
        ],
        compiler_params=params(40),
        cost_estimate=cost(10**10, 2 * 10**7),
        name="mesh_side",
    )(dst, halo, in_hbm(mesh_latent), in_hbm(enc_w), in_hbm(node_w))

    slot = jnp.arange(cap, dtype=jnp.int32)[:, None]
    live = slot < g2m_count
    sums, halo_out = pl.pallas_call(
        encode,
        out_shape=(
            pltpu.HBM((mesh_rows * parts, 128), F32),
            pltpu.HBM((halo_slots, width), BF16),
        ),
        in_specs=[SMEM, SMEM, VMEM, ANY, ANY, ANY, VMEM, VMEM, ANY, ANY, ANY, VMEM],
        out_specs=(ANY, ANY),
        scratch_shapes=[
            scratch((mesh_rows + cap) * parts),
            scratch(slots, width, BF16),
            scratch(slots * parts),
            scratch(HALO_STEP * parts),
            scratch(HALO_STEP * parts),
            scratch(halo_slots, width, BF16),
            scratch(width, width, BF16),
            scratch(width, width, BF16),
            scratch(width, width, BF16),
            scratch(halo_slots, width, BF16),
            sems(6 + halo_slots // HALO_STEP // 2),
        ],
        compiler_params=params(32),
        name="encode",
    )(
        jnp.where(live, dst, mesh_rows + slot).T.reshape(-1) * parts, halo.T.reshape(-1) * parts, arrived, in_hbm(mesh_term), in_hbm(own),
        in_hbm(own_halo), embed_in, embed_out, in_hbm(enc_w), folded, in_hbm(node_w), gains,
    )
    halo_in = lax.all_to_all(
        halo_out.reshape(peers, halo_cap, width), axes, split_axis=0, concat_axis=0, tiled=True
    ).reshape(halo_slots, width)

    remote = proc_src >= mesh_rows
    mesh_new, local = pl.pallas_call(
        local_terms,
        out_shape=(pltpu.HBM((mesh_rows, width), BF16), pltpu.HBM((edges, width), BF16)),
        in_specs=[SMEM, SMEM, ANY, ANY, ANY, ANY, VMEM, ANY],
        out_specs=(ANY, ANY),
        scratch_shapes=[
            scratch(mesh_rows * parts),
            scratch(mesh_rows, width, BF16),
            scratch(edges, width, BF16),
            scratch(mesh_rows, width, BF16),
            scratch(edges, width, BF16),
            scratch(width, width, BF16),
            pltpu.VMEM((3, width, width), BF16),
            scratch(mesh_rows * parts),
            scratch(mesh_rows * parts + 8),
            scratch(512 * parts),
            sems(2 + 2 * (mesh_rows // 512)),
            sems(2, edges // 512),
        ],
        compiler_params=params(40),
        cost_estimate=cost(2 * 10**10, 4 * 10**7),
        name="local_terms",
    )(
        proc_dst * parts,
        jnp.where(remote, mesh_rows, proc_src) * parts,
        in_hbm(sums),
        in_hbm(mesh_latent),
        in_hbm(node_w),
        in_hbm(proc_w),
        gains,
        in_hbm(edge_latent),
    )
    edge_new = pl.pallas_call(
        edge_update,
        out_shape=pltpu.HBM((edges, width), BF16),
        in_specs=[SMEM, VMEM, ANY, ANY, ANY, VMEM],
        out_specs=ANY,
        scratch_shapes=[
            pltpu.VMEM((2, width, width), BF16),
            scratch(edges, width, BF16),
            scratch(edges, width, BF16),
            scratch(edges, width, BF16),
            scratch(halo_slots * parts + 8),
            scratch(EDGE_STEP * parts),
            scratch(EDGE_STEP * parts),
            sems(1),
            sems(2, edges // EDGE_STEP // 2),
        ],
        compiler_params=params(28),
        name="edge_update",
    )(
        jnp.where(remote, proc_src - mesh_rows, halo_slots) * parts,
        halo_in,
        in_hbm(proc_w),
        in_hbm(edge_latent),
        in_hbm(local),
        gains,
    )
    return (mesh_new, edge_new)


def solution(mesh):
    rows = P(("band", "tile"), None)
    slots = P(("band", "tile"), None, None)
    flat = P(("band", "tile"))
    in_specs = (
        rows, P(), P(), rows, rows, P(), P(), P(), P(), slots, slots, rows, slots, flat, flat,
    )
    return jax.shard_map(
        shards, mesh=mesh, in_specs=in_specs, out_specs=(rows, rows), check_vma=False
    )
```

```python
import jax
import jax.numpy as jnp
from jax import lax
from jax.experimental import pallas as pl
from jax.experimental.pallas import tpu as pltpu
from jax.sharding import PartitionSpec as P

F32 = jnp.float32
BF16 = jnp.bfloat16
VMEM = pl.BlockSpec(memory_space=pltpu.VMEM)
SMEM = pl.BlockSpec(memory_space=pltpu.SMEM)
ANY = pl.BlockSpec(memory_space=pl.ANY)
STEP = 256
MESSAGE_STEP = 2048
HALO_STEP = 512
EDGE_STEP = 1024


def params(mebibytes):
    return pltpu.CompilerParams(vmem_limit_bytes=mebibytes * 2**20)


def in_hbm(array):
    return pltpu.with_memory_space_constraint(array, pltpu.HBM)


def dot(a, b):
    return jnp.dot(a, b, preferred_element_type=F32)


def silu(v):
    half = 0.5 * v
    return half + half * jnp.tanh(half)


def centre(weight):
    value = weight.astype(F32)
    return (value - jnp.mean(value, axis=-1, keepdims=True)).astype(BF16)


def norm(centred, gain):
    variance = jnp.mean(centred * centred, axis=-1, keepdims=True)
    return centred * lax.rsqrt(variance + 1e-05) * gain


def put_rows(table, start, value):
    rows, width = value.shape
    parts = width // 128
    for part in range(parts):
        table[pl.ds(start * parts + part, rows, stride=parts), :] = value[
            :, part * 128 : part * 128 + 128
        ]


def get_rows(table, start, rows, parts):
    return jnp.concatenate(
        [table[pl.ds(start * parts + part, rows, stride=parts), :] for part in range(parts)],
        axis=1,
    )


def slot_index(index, peer, inner, scale):
    cap = index.shape[0]
    return pl.multiple_of(index[inner % cap, peer + inner // cap] * scale, scale)


def pick_rows(at, table, target, base, rows, parts):
    for inner in range(rows):
        target[pl.ds(base * parts + inner * parts, parts), :] = table[pl.ds(at(inner), parts), :]


def pick_grid(
    index_in, grid_in, out_hbm, index, grid, table, picked, turned, out, index_sem, sems, out_sems
):
    features, rows = grid.shape
    slots = out.shape[0]
    step = STEP * 2

    def grid_copy(part):
        columns = pl.ds(pl.multiple_of(part * step, step), step)
        return pltpu.make_async_copy(grid_in.at[:, columns], grid.at[:, columns], sems.at[part])

    for part in range(rows // step):
        grid_copy(part).start()
    index_copy = pltpu.make_async_copy(index_in, index, index_sem)
    index_copy.start()

    @pl.loop(0, rows // STEP)
    def _(block):
        @pl.when(block % 2 == 0)
        def _():
            grid_copy(block // 2).wait()

        at = pl.multiple_of(block * STEP, STEP)
        turned[pl.ds(0, features), :] = grid[:, pl.ds(at, STEP)]
        put_rows(table, at, turned[...].T.astype(F32))

    index_copy.wait()
    step = 128
    span = slots // out_sems.shape[0]

    def out_copy(part):
        return pltpu.make_async_copy(
            piece(out, part, span), piece(out_hbm, part, span), out_sems.at[part]
        )

    for part in range(slots // span):

        @pl.loop(part * span // step, (part + 1) * span // step)
        def _(block):
            at = pl.multiple_of(block * step, step)
            first = block * (step // index.shape[0])
            pick_rows(lambda inner: slot_index(index, first, inner, 2), table, picked, at, step, 2)
            out[pl.ds(at, step), :] = get_rows(picked, at, step, 2)[:, :features].astype(BF16)

        out_copy(part).start()

    for part in range(slots // span):
        out_copy(part).wait()


def piece(ref, part, rows):
    return ref.at[pl.ds(pl.multiple_of(part * rows, rows), rows)]


def mesh_side(
    dst, halo, mesh, enc_w, node_w, embed_out,
    term_out, own_out, halo_out, folded_out, embed_centred, node_centred,
    table, copies, picked, picked_too, own, terms, halves, latents, w_enc, w_node, sems,
):
    rows = mesh.shape[0]
    slots = halo_out.shape[0]
    step = 512
    chunks = rows // step
    weights = [
        pltpu.make_async_copy(enc_w.at[pl.ds(1, 2)], w_enc, sems.at[0]),
        pltpu.make_async_copy(node_w, w_node, sems.at[1]),
    ]
    for copy in weights:
        copy.start()

    def latent_copy(part):
        return pltpu.make_async_copy(
            piece(mesh, part, step), piece(latents, part, step), sems.at[2 + part]
        )

    for part in range(chunks):
        latent_copy(part).start()
    for copy in weights:
        copy.wait()

    @pl.loop(0, chunks)
    def _(block):
        at = pl.multiple_of(block * step, step)
        latent_copy(block).wait()
        value = latents[pl.ds(at, step), :]
        put_rows(table, at, dot(value, w_enc[0]))
        put_rows(own, at, dot(value, w_node[0]))
        put_rows(copies, at, value.astype(F32))

    outs = [pltpu.make_async_copy(own, own_out, sems.at[0])]
    outs[0].start()
    folded_out[...] = dot(w_enc[1], w_node[1]).astype(BF16)
    embed_centred[...] = centre(embed_out[...])
    node_centred[...] = centre(w_node[2])
    step = 64
    parts = 4
    span = slots // parts
    for part in range(parts):

        @pl.loop(part * span // step, (part + 1) * span // step)
        def _(block):
            at = pl.multiple_of(block * step, step)
            pick_rows(lambda inner: slot_index(dst, block * (step // dst.shape[0]), inner, 4), table, picked_too, at, step, 4)
            pick_rows(lambda inner: slot_index(halo, block * (step // halo.shape[0]), inner, 4), copies, picked, at, step, 4)
            terms[pl.ds(at, step), :] = get_rows(picked_too, at, step, 4).astype(BF16)
            halves[pl.ds(at, step), :] = get_rows(picked, at, step, 4).astype(BF16)

        outs.append(
            pltpu.make_async_copy(
                piece(terms, part, span), piece(term_out, part, span), sems.at[2 + part]
            )
        )
        outs[-1].start()
    outs.append(pltpu.make_async_copy(halves, halo_out, sems.at[1]))
    outs[-1].start()
    for copy in outs:
        copy.wait()


def node_update(pre, own, w_out, gain):
    return (own.astype(F32) + norm(dot(silu(pre).astype(BF16), w_out), gain)).astype(BF16)


def encode(
    target, halo, rows_in, mesh_term, own, own_halo, embed_in, embed_out, enc_w, folded, node_centred,
    gains, sums_out, halo_out,
    sums, terms, sent, first, second, halves, w_grid, w_message, w_out, halo_rows, sems,
):
    slots = rows_in.shape[0]
    mesh_rows = own.shape[0]
    blocks = slots // HALO_STEP
    copies = [
        pltpu.make_async_copy(enc_w.at[0], w_grid, sems.at[0]),
        pltpu.make_async_copy(folded, w_message, sems.at[1]),
        pltpu.make_async_copy(mesh_term, terms, sems.at[2]),
        pltpu.make_async_copy(own, sums.at[pl.ds(0, mesh_rows)], sems.at[3]),
        pltpu.make_async_copy(node_centred, w_out, sems.at[4]),
        pltpu.make_async_copy(own_halo, halves, sems.at[5]),
    ]
    for copy in copies:
        copy.start()
    spare = sums.shape[0] - mesh_rows
    sums[pl.ds(mesh_rows, spare), :] = jnp.zeros((spare, 128), F32)
    for copy in copies[:3]:
        copy.wait()
    step = MESSAGE_STEP

    @pl.loop(0, slots // step)
    def _(block):
        at = pl.multiple_of(block * step, step)
        hidden = silu(dot(rows_in[pl.ds(at, step), :], embed_in[...])).astype(BF16)
        latent = norm(dot(hidden, embed_out[...]), gains[0:1, :]).astype(BF16)
        pre = dot(latent, w_grid[...]) + terms[pl.ds(at, step), :].astype(F32)
        put_rows(sent, at, dot(silu(pre).astype(BF16), w_message[...]))

    copies[3].wait()

    @pl.loop(0, slots // 32)
    def _(block):
        for inner in range(32):
            row = block * 32 + inner
            to = pl.ds(pl.multiple_of(target[row], 4), 4)
            sums[to, :] = sums[to, :] + sent[pl.ds(pl.multiple_of(row * 4, 4), 4), :]

    sums_copy = pltpu.make_async_copy(sums.at[pl.ds(0, mesh_rows)], sums_out, sems.at[3])
    sums_copy.start()
    for copy in copies[4:]:
        copy.wait()

    def pick(block, into):
        at = block * HALO_STEP
        pick_rows(
            lambda inner: pl.multiple_of(halo[at + inner], 4), sums, into, 0, HALO_STEP, 4
        )

    def update(block, source):
        at = pl.multiple_of(block * HALO_STEP, HALO_STEP)
        halo_rows[pl.ds(at, HALO_STEP), :] = node_update(
            get_rows(source, 0, HALO_STEP, 4), halves[pl.ds(at, HALO_STEP), :], w_out[...], gains[1:2, :]
        )

    pick(0, first)

    def halo_copy(pair):
        return pltpu.make_async_copy(
            piece(halo_rows, pair, HALO_STEP * 2), piece(halo_out, pair, HALO_STEP * 2), sems.at[6 + pair]
        )

    @pl.loop(0, blocks // 2)
    def _(pair):
        pick(pair * 2 + 1, second)
        update(pair * 2, first)
        pick(jnp.minimum(pair * 2 + 2, blocks - 1), first)
        update(pair * 2 + 1, second)
        halo_copy(pair).start()

    sums_copy.wait()
    for pair in range(blocks // 2):
        halo_copy(pair).wait()


def local_terms(
    dst, src, sums_in, mesh, node_centred, proc_w, gains, edges_in, mesh_out, out, proc_centred,
    sums, latents, edges, new, local, w_node, w_proc, receivers, senders, picked, sems, edge_sems,
):
    rows = mesh.shape[0]
    step = 512
    chunks = rows // step
    edge_chunks = edges.shape[0] // step
    weights = [
        pltpu.make_async_copy(node_centred, w_node, sems.at[0]),
        pltpu.make_async_copy(proc_w, w_proc, sems.at[1]),
    ]

    def sums_copy(part):
        return pltpu.make_async_copy(
            piece(sums_in, part, step * 4), piece(sums, part, step * 4), sems.at[2 + part]
        )

    def latent_copy(part):
        return pltpu.make_async_copy(
            piece(mesh, part, step), piece(latents, part, step), sems.at[2 + chunks + part]
        )

    def new_copy(part):
        return pltpu.make_async_copy(
            piece(new, part, step), piece(mesh_out, part, step), sems.at[2 + part]
        )

    def edge_copy(part):
        return pltpu.make_async_copy(
            piece(edges_in, part, step), piece(edges, part, step), edge_sems.at[0, part]
        )

    def local_copy(part):
        return pltpu.make_async_copy(
            piece(local, part, step), piece(out, part, step), edge_sems.at[1, part]
        )

    for copy in weights:
        copy.start()
    for part in range(chunks):
        sums_copy(part).start()
        latent_copy(part).start()
    for part in range(edge_chunks):
        edge_copy(part).start()
    senders[pl.ds(rows * 4, 8), :] = jnp.zeros((8, 128), F32)
    for copy in weights:
        copy.wait()
    proc_centred[...] = centre(w_proc[3])

    @pl.loop(0, chunks)
    def _(block):
        at = pl.multiple_of(block * step, step)
        sums_copy(block).wait()
        latent_copy(block).wait()
        value = node_update(
            get_rows(sums, at, step, 4), latents[pl.ds(at, step), :], w_node[...], gains[1:2, :]
        )
        new[pl.ds(at, step), :] = value
        put_rows(receivers, at, dot(value, w_proc[1]))
        put_rows(senders, at, dot(value, w_proc[2]))
        new_copy(block).start()

    @pl.loop(0, edge_chunks)
    def _(block):
        start = pl.multiple_of(block * step, step)
        edge_copy(block).wait()

        @pl.loop(0, step // 32)
        def _(group):
            for inner in range(32):
                row = group * 32 + inner
                one = pl.multiple_of(dst[start + row], 4)
                two = pl.multiple_of(src[start + row], 4)
                picked[pl.ds(pl.multiple_of(row * 4, 4), 4), :] = (
                    receivers[pl.ds(one, 4), :] + senders[pl.ds(two, 4), :]
                )

        here = pl.ds(start, step)
        value = dot(edges[here, :], w_proc[0]) + get_rows(picked, 0, step, 4)
        local[here, :] = value.astype(BF16)
        local_copy(block).start()

    for part in range(chunks):
        new_copy(part).wait()
    for part in range(edge_chunks):
        local_copy(part).wait()


def edge_update(
    src, halo, proc_w, proc_centred, edges_in, local_in, gains, out,
    w_proc, edges, local, new, senders, first, second, sems, edge_sems,
):
    rows = halo.shape[0]
    step = 1024
    chunks = rows // step
    edge_step = EDGE_STEP * 2
    edge_chunks = edges.shape[0] // edge_step
    last = src.shape[0] // EDGE_STEP - 1
    weights = pltpu.make_async_copy(proc_w.at[2], w_proc.at[0], sems.at[0])
    last_weight = pltpu.make_async_copy(proc_centred, w_proc.at[1], sems.at[1])

    def edge_copy(part):
        return pltpu.make_async_copy(
            piece(edges_in, part, edge_step), piece(edges, part, edge_step), edge_sems.at[0, part]
        )

    def local_copy(part):
        return pltpu.make_async_copy(
            piece(local_in, part, edge_step), piece(local, part, edge_step), edge_sems.at[1, part]
        )

    def new_copy(part):
        return pltpu.make_async_copy(
            piece(new, part, edge_step), piece(out, part, edge_step), edge_sems.at[0, part]
        )

    weights.start()
    last_weight.start()
    for part in range(edge_chunks):
        local_copy(part).start()
        edge_copy(part).start()
    senders[pl.ds(rows * 4, 8), :] = jnp.zeros((8, 128), F32)
    weights.wait()

    @pl.loop(0, chunks)
    def _(block):
        at = pl.multiple_of(block * step, step)
        put_rows(senders, at, dot(halo[pl.ds(at, step), :], w_proc[0]))

    def pick(block, into):
        at = block * EDGE_STEP
        pick_rows(lambda inner: pl.multiple_of(src[at + inner], 4), senders, into, 0, EDGE_STEP, 4)

    def update(block, source):
        here = pl.ds(pl.multiple_of(block * EDGE_STEP, EDGE_STEP), EDGE_STEP)
        hidden = silu(local[here, :].astype(F32) + get_rows(source, 0, EDGE_STEP, 4)).astype(BF16)
        change = norm(dot(hidden, w_proc[1]), gains[2:3, :])
        new[here, :] = (edges[here, :].astype(F32) + change).astype(BF16)

    last_weight.wait()
    pick(0, first)

    @pl.loop(0, edge_chunks)
    def _(pair):
        edge_copy(pair).wait()
        local_copy(pair).wait()
        pick(pair * 2 + 1, second)
        update(pair * 2, first)
        pick(jnp.minimum(pair * 2 + 2, last), first)
        update(pair * 2 + 1, second)
        new_copy(pair).start()

    for part in range(edge_chunks):
        new_copy(part).wait()


def shards(
    grid_in,
    embed_in,
    embed_out,
    mesh_latent,
    edge_latent,
    enc_w,
    node_w,
    proc_w,
    gains,
    g2m_src,
    g2m_dst,
    g2m_count,
    halo_rows,
    proc_dst,
    proc_src,
):
    axes = ("band", "tile")
    peers = lax.axis_size("band") * lax.axis_size("tile")
    grid_rows, features = grid_in.shape
    mesh_rows, width = mesh_latent.shape
    edges = edge_latent.shape[0]
    cap = g2m_src.shape[2]
    halo_cap = halo_rows.shape[2]
    slots = peers * cap
    halo_slots = peers * halo_cap
    parts = width // 128

    def full(rows, columns, dtype):
        return jax.ShapeDtypeStruct((rows, columns), dtype)

    def scratch(rows, columns=128, dtype=F32):
        return pltpu.VMEM((rows, columns), dtype)

    def cost(flops, moved):
        return pl.CostEstimate(flops=flops, bytes_accessed=moved, transcendentals=0)

    def sems(*counts):
        return pltpu.SemaphoreType.DMA(counts)

    outgoing = pl.pallas_call(
        pick_grid,
        out_shape=pltpu.HBM((slots, features), BF16),
        in_specs=[ANY, ANY],
        out_specs=ANY,
        scratch_shapes=[
            pltpu.SMEM((cap, peers), jnp.int32),
            scratch(features, grid_rows, BF16),
            scratch(grid_rows * 2),
            scratch(slots * 2),
            scratch(256, STEP, BF16),
            scratch(slots, features, BF16),
            pltpu.SemaphoreType.DMA,
            sems(grid_rows // (STEP * 2)),
            sems(4),
        ],
        compiler_params=params(14),
        name="pick_grid",
    )(in_hbm(g2m_src[0].T), in_hbm(grid_in.T))
    arrived = lax.all_to_all(
        outgoing.reshape(peers, cap, features), axes, split_axis=0, concat_axis=0, tiled=True
    ).reshape(slots, features)

    dst = g2m_dst[0].T
    halo = halo_rows[0].T
    mesh_term, own, own_halo, folded, embed_centred, node_centred = pl.pallas_call(
        mesh_side,
        out_shape=(
            pltpu.HBM((slots, width), BF16),
            pltpu.HBM((mesh_rows * parts, 128), F32),
            pltpu.HBM((halo_slots, width), BF16),
            full(width, width, BF16),
            full(width, width, BF16),
            full(width, width, BF16),
        ),
        in_specs=[SMEM, SMEM, ANY, ANY, ANY, VMEM],
        out_specs=(ANY, ANY, ANY, VMEM, VMEM, VMEM),
        scratch_shapes=[
            scratch(mesh_rows * parts),
            scratch(mesh_rows * parts),
            scratch(halo_slots * parts),
            scratch(slots * parts),
            scratch(mesh_rows * parts),
            scratch(slots, width, BF16),
            scratch(halo_slots, width, BF16),
            scratch(mesh_rows, width, BF16),
            pltpu.VMEM((2, width, width), BF16),
            pltpu.VMEM((3, width, width), BF16),
            sems(2 + mesh_rows // 512),
        ],
        compiler_params=params(40),
        cost_estimate=cost(10**10, 2 * 10**7),
        name="mesh_side",
    )(dst, halo, in_hbm(mesh_latent), in_hbm(enc_w), in_hbm(node_w), embed_out)

    slot = jnp.arange(cap, dtype=jnp.int32)[:, None]
    live = slot < g2m_count
    sums, halo_out = pl.pallas_call(
        encode,
        out_shape=(
            pltpu.HBM((mesh_rows * parts, 128), F32),
            pltpu.HBM((halo_slots, width), BF16),
        ),
        in_specs=[SMEM, SMEM, VMEM, ANY, ANY, ANY, VMEM, VMEM, ANY, ANY, ANY, VMEM],
        out_specs=(ANY, ANY),
        scratch_shapes=[
            scratch((mesh_rows + cap) * parts),
            scratch(slots, width, BF16),
            scratch(slots * parts),
            scratch(HALO_STEP * parts),
            scratch(HALO_STEP * parts),
            scratch(halo_slots, width, BF16),
            scratch(width, width, BF16),
            scratch(width, width, BF16),
            scratch(width, width, BF16),
            scratch(halo_slots, width, BF16),
            sems(6 + halo_slots // HALO_STEP // 2),
        ],
        compiler_params=params(32),
        name="encode",
    )(
        jnp.where(live, dst, mesh_rows + slot).T.reshape(-1) * parts, halo.T.reshape(-1) * parts, arrived, in_hbm(mesh_term), in_hbm(own),
        in_hbm(own_halo), embed_in, embed_centred, in_hbm(enc_w), folded, node_centred, gains,
    )
    halo_in = lax.all_to_all(
        halo_out.reshape(peers, halo_cap, width), axes, split_axis=0, concat_axis=0, tiled=True
    ).reshape(halo_slots, width)

    remote = proc_src >= mesh_rows
    mesh_new, local, proc_centred = pl.pallas_call(
        local_terms,
        out_shape=(
            pltpu.HBM((mesh_rows, width), BF16),
            pltpu.HBM((edges, width), BF16),
            pltpu.HBM((width, width), BF16),
        ),
        in_specs=[SMEM, SMEM, ANY, ANY, ANY, ANY, VMEM, ANY],
        out_specs=(ANY, ANY, VMEM),
        scratch_shapes=[
            scratch(mesh_rows * parts),
            scratch(mesh_rows, width, BF16),
            scratch(edges, width, BF16),
            scratch(mesh_rows, width, BF16),
            scratch(edges, width, BF16),
            scratch(width, width, BF16),
            pltpu.VMEM((4, width, width), BF16),
            scratch(mesh_rows * parts),
            scratch(mesh_rows * parts + 8),
            scratch(512 * parts),
            sems(2 + 2 * (mesh_rows // 512)),
            sems(2, edges // 512),
        ],
        compiler_params=params(40),
        cost_estimate=cost(2 * 10**10, 4 * 10**7),
        name="local_terms",
    )(
        proc_dst * parts,
        jnp.where(remote, mesh_rows, proc_src) * parts,
        in_hbm(sums),
        in_hbm(mesh_latent),
        node_centred,
        in_hbm(proc_w),
        gains,
        in_hbm(edge_latent),
    )
    edge_new = pl.pallas_call(
        edge_update,
        out_shape=pltpu.HBM((edges, width), BF16),
        in_specs=[SMEM, VMEM, ANY, ANY, ANY, ANY, VMEM],
        out_specs=ANY,
        scratch_shapes=[
            pltpu.VMEM((2, width, width), BF16),
            scratch(edges, width, BF16),
            scratch(edges, width, BF16),
            scratch(edges, width, BF16),
            scratch(halo_slots * parts + 8),
            scratch(EDGE_STEP * parts),
            scratch(EDGE_STEP * parts),
            sems(2),
            sems(2, edges // EDGE_STEP // 2),
        ],
        compiler_params=params(28),
        name="edge_update",
    )(
        jnp.where(remote, proc_src - mesh_rows, halo_slots) * parts,
        halo_in,
        in_hbm(proc_w),
        in_hbm(proc_centred),
        in_hbm(edge_latent),
        in_hbm(local),
        gains,
    )
    return (mesh_new, edge_new)


def solution(mesh):
    rows = P(("band", "tile"), None)
    slots = P(("band", "tile"), None, None)
    flat = P(("band", "tile"))
    in_specs = (
        rows, P(), P(), rows, rows, P(), P(), P(), P(), slots, slots, rows, slots, flat, flat,
    )
    return jax.shard_map(
        shards, mesh=mesh, in_specs=in_specs, out_specs=(rows, rows), check_vma=False
    )
```

```python
import jax
import jax.numpy as jnp
from jax import lax
from jax.experimental import pallas as pl
from jax.experimental.pallas import tpu as pltpu
from jax.sharding import PartitionSpec as P

F32 = jnp.float32
BF16 = jnp.bfloat16
VMEM = pl.BlockSpec(memory_space=pltpu.VMEM)
SMEM = pl.BlockSpec(memory_space=pltpu.SMEM)
ANY = pl.BlockSpec(memory_space=pl.ANY)
STEP = 256
MESSAGE_STEP = 2048
HALO_STEP = 512
EDGE_STEP = 1024


def params(mebibytes):
    return pltpu.CompilerParams(vmem_limit_bytes=mebibytes * 2**20)


def in_hbm(array):
    return pltpu.with_memory_space_constraint(array, pltpu.HBM)


def dot(a, b):
    return jnp.dot(a, b, preferred_element_type=F32)


def silu_of_double(half):
    return half + half * jnp.tanh(half)


def silu(v):
    return silu_of_double(0.5 * v)


def centre(weight):
    value = weight.astype(F32)
    return (value - jnp.mean(value, axis=-1, keepdims=True)).astype(BF16)


def norm(centred, gain):
    variance = jnp.mean(centred * centred, axis=-1, keepdims=True)
    return centred * lax.rsqrt(variance + 1e-05) * gain


def put_rows(table, start, value):
    rows, width = value.shape
    parts = width // 128
    for part in range(parts):
        table[pl.ds(start * parts + part, rows, stride=parts), :] = value[
            :, part * 128 : part * 128 + 128
        ]


def get_rows(table, start, rows, parts):
    return jnp.concatenate(
        [table[pl.ds(start * parts + part, rows, stride=parts), :] for part in range(parts)],
        axis=1,
    )


def slot_index(index, peer, inner, scale):
    cap = index.shape[0]
    return pl.multiple_of(index[inner % cap, peer + inner // cap] * scale, scale)


def pick_rows(at, table, target, base, rows, parts):
    for inner in range(rows):
        target[pl.ds(base * parts + inner * parts, parts), :] = table[pl.ds(at(inner), parts), :]


def pick_grid(
    index_in, grid_in, out_hbm, index, grid, table, picked, turned, out, index_sem, sems, out_sems
):
    features, rows = grid.shape
    slots = out.shape[0]
    step = STEP * 2

    def grid_copy(part):
        columns = pl.ds(pl.multiple_of(part * step, step), step)
        return pltpu.make_async_copy(grid_in.at[:, columns], grid.at[:, columns], sems.at[part])

    for part in range(rows // step):
        grid_copy(part).start()
    index_copy = pltpu.make_async_copy(index_in, index, index_sem)
    index_copy.start()

    @pl.loop(0, rows // STEP)
    def _(block):
        @pl.when(block % 2 == 0)
        def _():
            grid_copy(block // 2).wait()

        at = pl.multiple_of(block * STEP, STEP)
        turned[pl.ds(0, features), :] = grid[:, pl.ds(at, STEP)]
        put_rows(table, at, turned[...].T.astype(F32))

    index_copy.wait()
    step = 128
    span = slots // out_sems.shape[0]

    def out_copy(part):
        return pltpu.make_async_copy(
            piece(out, part, span), piece(out_hbm, part, span), out_sems.at[part]
        )

    for part in range(slots // span):

        @pl.loop(part * span // step, (part + 1) * span // step)
        def _(block):
            at = pl.multiple_of(block * step, step)
            first = block * (step // index.shape[0])
            pick_rows(lambda inner: slot_index(index, first, inner, 2), table, picked, at, step, 2)
            out[pl.ds(at, step), :] = get_rows(picked, at, step, 2)[:, :features].astype(BF16)

        out_copy(part).start()

    for part in range(slots // span):
        out_copy(part).wait()


def piece(ref, part, rows):
    return ref.at[pl.ds(pl.multiple_of(part * rows, rows), rows)]


def mesh_side(
    dst, halo, mesh, enc_w, node_w, embed_out,
    term_out, own_out, halo_out, folded_out, embed_centred, node_centred,
    table, copies, picked, picked_too, own, terms, halves, latents, w_enc, w_node, sems,
):
    rows = mesh.shape[0]
    slots = halo_out.shape[0]
    step = 512
    chunks = rows // step
    weights = [
        pltpu.make_async_copy(enc_w.at[pl.ds(1, 2)], w_enc, sems.at[0]),
        pltpu.make_async_copy(node_w, w_node, sems.at[1]),
    ]
    for copy in weights:
        copy.start()

    def latent_copy(part):
        return pltpu.make_async_copy(
            piece(mesh, part, step), piece(latents, part, step), sems.at[2 + part]
        )

    for part in range(chunks):
        latent_copy(part).start()
    for copy in weights:
        copy.wait()

    @pl.loop(0, chunks)
    def _(block):
        at = pl.multiple_of(block * step, step)
        latent_copy(block).wait()
        value = latents[pl.ds(at, step), :]
        put_rows(table, at, dot(value, w_enc[0]))
        put_rows(own, at, 0.5 * dot(value, w_node[0]))
        put_rows(copies, at, value.astype(F32))

    outs = [pltpu.make_async_copy(own, own_out, sems.at[0])]
    outs[0].start()
    folded_out[...] = (0.5 * dot(w_enc[1], w_node[1])).astype(BF16)
    embed_centred[...] = centre(embed_out[...])
    node_centred[...] = centre(w_node[2])
    step = 64
    parts = 4
    span = slots // parts
    for part in range(parts):

        @pl.loop(part * span // step, (part + 1) * span // step)
        def _(block):
            at = pl.multiple_of(block * step, step)
            pick_rows(lambda inner: slot_index(dst, block * (step // dst.shape[0]), inner, 4), table, picked_too, at, step, 4)
            pick_rows(lambda inner: slot_index(halo, block * (step // halo.shape[0]), inner, 4), copies, picked, at, step, 4)
            terms[pl.ds(at, step), :] = get_rows(picked_too, at, step, 4).astype(BF16)
            halves[pl.ds(at, step), :] = get_rows(picked, at, step, 4).astype(BF16)

        outs.append(
            pltpu.make_async_copy(
                piece(terms, part, span), piece(term_out, part, span), sems.at[2 + part]
            )
        )
        outs[-1].start()
    outs.append(pltpu.make_async_copy(halves, halo_out, sems.at[1]))
    outs[-1].start()
    for copy in outs:
        copy.wait()


def node_update(half, own, w_out, gain):
    return (own.astype(F32) + norm(dot(silu_of_double(half).astype(BF16), w_out), gain)).astype(BF16)


def encode(
    target, halo, rows_in, mesh_term, own, own_halo, embed_in, embed_out, enc_w, folded, node_centred,
    gains, sums_out, halo_out,
    sums, terms, sent, first, second, halves, w_grid, w_message, w_out, halo_rows, sems,
):
    slots = rows_in.shape[0]
    mesh_rows = own.shape[0]
    blocks = slots // HALO_STEP
    copies = [
        pltpu.make_async_copy(enc_w.at[0], w_grid, sems.at[0]),
        pltpu.make_async_copy(folded, w_message, sems.at[1]),
        pltpu.make_async_copy(mesh_term, terms, sems.at[2]),
        pltpu.make_async_copy(own, sums.at[pl.ds(0, mesh_rows)], sems.at[3]),
        pltpu.make_async_copy(node_centred, w_out, sems.at[4]),
        pltpu.make_async_copy(own_halo, halves, sems.at[5]),
    ]
    for copy in copies:
        copy.start()
    spare = sums.shape[0] - mesh_rows
    sums[pl.ds(mesh_rows, spare), :] = jnp.zeros((spare, 128), F32)
    for copy in copies[:3]:
        copy.wait()
    step = MESSAGE_STEP

    @pl.loop(0, slots // step)
    def _(block):
        at = pl.multiple_of(block * step, step)
        hidden = silu(dot(rows_in[pl.ds(at, step), :], embed_in[...])).astype(BF16)
        latent = norm(dot(hidden, embed_out[...]), gains[0:1, :]).astype(BF16)
        pre = dot(latent, w_grid[...]) + terms[pl.ds(at, step), :].astype(F32)
        put_rows(sent, at, dot(silu(pre).astype(BF16), w_message[...]))

    copies[3].wait()

    @pl.loop(0, slots // 32)
    def _(block):
        for inner in range(32):
            row = block * 32 + inner
            to = pl.ds(pl.multiple_of(target[row], 4), 4)
            sums[to, :] = sums[to, :] + sent[pl.ds(pl.multiple_of(row * 4, 4), 4), :]

    sums_copy = pltpu.make_async_copy(sums.at[pl.ds(0, mesh_rows)], sums_out, sems.at[3])
    sums_copy.start()
    for copy in copies[4:]:
        copy.wait()

    def pick(block, into):
        at = block * HALO_STEP
        pick_rows(
            lambda inner: pl.multiple_of(halo[at + inner], 4), sums, into, 0, HALO_STEP, 4
        )

    def update(block, source):
        at = pl.multiple_of(block * HALO_STEP, HALO_STEP)
        halo_rows[pl.ds(at, HALO_STEP), :] = node_update(
            get_rows(source, 0, HALO_STEP, 4), halves[pl.ds(at, HALO_STEP), :], w_out[...], gains[1:2, :]
        )

    pick(0, first)

    def halo_copy(pair):
        return pltpu.make_async_copy(
            piece(halo_rows, pair, HALO_STEP * 2), piece(halo_out, pair, HALO_STEP * 2), sems.at[6 + pair]
        )

    @pl.loop(0, blocks // 2)
    def _(pair):
        pick(pair * 2 + 1, second)
        update(pair * 2, first)
        pick(jnp.minimum(pair * 2 + 2, blocks - 1), first)
        update(pair * 2 + 1, second)
        halo_copy(pair).start()

    sums_copy.wait()
    for pair in range(blocks // 2):
        halo_copy(pair).wait()


def local_terms(
    dst, src, sums_in, mesh, node_centred, proc_w, gains, edges_in, mesh_out, out, proc_centred,
    sums, latents, edges, new, local, w_node, w_proc, receivers, senders, picked, sems, edge_sems,
):
    rows = mesh.shape[0]
    step = 512
    chunks = rows // step
    edge_chunks = edges.shape[0] // step
    weights = [
        pltpu.make_async_copy(node_centred, w_node, sems.at[0]),
        pltpu.make_async_copy(proc_w, w_proc, sems.at[1]),
    ]

    def sums_copy(part):
        return pltpu.make_async_copy(
            piece(sums_in, part, step * 4), piece(sums, part, step * 4), sems.at[2 + part]
        )

    def latent_copy(part):
        return pltpu.make_async_copy(
            piece(mesh, part, step), piece(latents, part, step), sems.at[2 + chunks + part]
        )

    def new_copy(part):
        return pltpu.make_async_copy(
            piece(new, part, step), piece(mesh_out, part, step), sems.at[2 + part]
        )

    def edge_copy(part):
        return pltpu.make_async_copy(
            piece(edges_in, part, step), piece(edges, part, step), edge_sems.at[0, part]
        )

    def local_copy(part):
        return pltpu.make_async_copy(
            piece(local, part, step), piece(out, part, step), edge_sems.at[1, part]
        )

    for copy in weights:
        copy.start()
    for part in range(chunks):
        sums_copy(part).start()
        latent_copy(part).start()
    for part in range(edge_chunks):
        edge_copy(part).start()
    senders[pl.ds(rows * 4, 8), :] = jnp.zeros((8, 128), F32)
    for copy in weights:
        copy.wait()
    proc_centred[...] = centre(w_proc[3])

    @pl.loop(0, chunks)
    def _(block):
        at = pl.multiple_of(block * step, step)
        sums_copy(block).wait()
        latent_copy(block).wait()
        value = node_update(
            get_rows(sums, at, step, 4), latents[pl.ds(at, step), :], w_node[...], gains[1:2, :]
        )
        new[pl.ds(at, step), :] = value
        put_rows(receivers, at, dot(value, w_proc[1]))
        put_rows(senders, at, dot(value, w_proc[2]))
        new_copy(block).start()

    @pl.loop(0, edge_chunks)
    def _(block):
        start = pl.multiple_of(block * step, step)
        edge_copy(block).wait()

        @pl.loop(0, step // 32)
        def _(group):
            for inner in range(32):
                row = group * 32 + inner
                one = pl.multiple_of(dst[start + row], 4)
                two = pl.multiple_of(src[start + row], 4)
                picked[pl.ds(pl.multiple_of(row * 4, 4), 4), :] = (
                    receivers[pl.ds(one, 4), :] + senders[pl.ds(two, 4), :]
                )

        here = pl.ds(start, step)
        value = dot(edges[here, :], w_proc[0]) + get_rows(picked, 0, step, 4)
        local[here, :] = (0.5 * value).astype(BF16)
        local_copy(block).start()

    for part in range(chunks):
        new_copy(part).wait()
    for part in range(edge_chunks):
        local_copy(part).wait()


def edge_update(
    src, halo, proc_w, proc_centred, edges_in, local_in, gains, out,
    w_proc, edges, local, new, senders, first, second, sems, edge_sems,
):
    rows = halo.shape[0]
    step = 1024
    chunks = rows // step
    edge_step = EDGE_STEP * 2
    edge_chunks = edges.shape[0] // edge_step
    last = src.shape[0] // EDGE_STEP - 1
    weights = pltpu.make_async_copy(proc_w.at[2], w_proc.at[0], sems.at[0])
    last_weight = pltpu.make_async_copy(proc_centred, w_proc.at[1], sems.at[1])

    def edge_copy(part):
        return pltpu.make_async_copy(
            piece(edges_in, part, edge_step), piece(edges, part, edge_step), edge_sems.at[0, part]
        )

    def local_copy(part):
        return pltpu.make_async_copy(
            piece(local_in, part, edge_step), piece(local, part, edge_step), edge_sems.at[1, part]
        )

    def new_copy(part):
        return pltpu.make_async_copy(
            piece(new, part, edge_step), piece(out, part, edge_step), edge_sems.at[0, part]
        )

    weights.start()
    last_weight.start()
    for part in range(edge_chunks):
        local_copy(part).start()
        edge_copy(part).start()
    senders[pl.ds(rows * 4, 8), :] = jnp.zeros((8, 128), F32)
    weights.wait()

    @pl.loop(0, chunks)
    def _(block):
        at = pl.multiple_of(block * step, step)
        put_rows(senders, at, 0.5 * dot(halo[pl.ds(at, step), :], w_proc[0]))

    def pick(block, into):
        at = block * EDGE_STEP
        pick_rows(lambda inner: pl.multiple_of(src[at + inner], 4), senders, into, 0, EDGE_STEP, 4)

    def update(block, source):
        here = pl.ds(pl.multiple_of(block * EDGE_STEP, EDGE_STEP), EDGE_STEP)
        hidden = silu_of_double(local[here, :].astype(F32) + get_rows(source, 0, EDGE_STEP, 4)).astype(BF16)
        change = norm(dot(hidden, w_proc[1]), gains[2:3, :])
        new[here, :] = (edges[here, :].astype(F32) + change).astype(BF16)

    last_weight.wait()
    pick(0, first)

    @pl.loop(0, edge_chunks)
    def _(pair):
        edge_copy(pair).wait()
        local_copy(pair).wait()
        pick(pair * 2 + 1, second)
        update(pair * 2, first)
        pick(jnp.minimum(pair * 2 + 2, last), first)
        update(pair * 2 + 1, second)
        new_copy(pair).start()

    for part in range(edge_chunks):
        new_copy(part).wait()


def shards(
    grid_in,
    embed_in,
    embed_out,
    mesh_latent,
    edge_latent,
    enc_w,
    node_w,
    proc_w,
    gains,
    g2m_src,
    g2m_dst,
    g2m_count,
    halo_rows,
    proc_dst,
    proc_src,
):
    axes = ("band", "tile")
    peers = lax.axis_size("band") * lax.axis_size("tile")
    grid_rows, features = grid_in.shape
    mesh_rows, width = mesh_latent.shape
    edges = edge_latent.shape[0]
    cap = g2m_src.shape[2]
    halo_cap = halo_rows.shape[2]
    slots = peers * cap
    halo_slots = peers * halo_cap
    parts = width // 128

    def full(rows, columns, dtype):
        return jax.ShapeDtypeStruct((rows, columns), dtype)

    def scratch(rows, columns=128, dtype=F32):
        return pltpu.VMEM((rows, columns), dtype)

    def cost(flops, moved):
        return pl.CostEstimate(flops=flops, bytes_accessed=moved, transcendentals=0)

    def sems(*counts):
        return pltpu.SemaphoreType.DMA(counts)

    outgoing = pl.pallas_call(
        pick_grid,
        out_shape=pltpu.HBM((slots, features), BF16),
        in_specs=[ANY, ANY],
        out_specs=ANY,
        scratch_shapes=[
            pltpu.SMEM((cap, peers), jnp.int32),
            scratch(features, grid_rows, BF16),
            scratch(grid_rows * 2),
            scratch(slots * 2),
            scratch(256, STEP, BF16),
            scratch(slots, features, BF16),
            pltpu.SemaphoreType.DMA,
            sems(grid_rows // (STEP * 2)),
            sems(4),
        ],
        compiler_params=params(14),
        name="pick_grid",
    )(in_hbm(g2m_src[0].T), in_hbm(grid_in.T))
    arrived = lax.all_to_all(
        outgoing.reshape(peers, cap, features), axes, split_axis=0, concat_axis=0, tiled=True
    ).reshape(slots, features)

    dst = g2m_dst[0].T
    halo = halo_rows[0].T
    mesh_term, own, own_halo, folded, embed_centred, node_centred = pl.pallas_call(
        mesh_side,
        out_shape=(
            pltpu.HBM((slots, width), BF16),
            pltpu.HBM((mesh_rows * parts, 128), F32),
            pltpu.HBM((halo_slots, width), BF16),
            full(width, width, BF16),
            full(width, width, BF16),
            full(width, width, BF16),
        ),
        in_specs=[SMEM, SMEM, ANY, ANY, ANY, VMEM],
        out_specs=(ANY, ANY, ANY, VMEM, VMEM, VMEM),
        scratch_shapes=[
            scratch(mesh_rows * parts),
            scratch(mesh_rows * parts),
            scratch(halo_slots * parts),
            scratch(slots * parts),
            scratch(mesh_rows * parts),
            scratch(slots, width, BF16),
            scratch(halo_slots, width, BF16),
            scratch(mesh_rows, width, BF16),
            pltpu.VMEM((2, width, width), BF16),
            pltpu.VMEM((3, width, width), BF16),
            sems(2 + mesh_rows // 512),
        ],
        compiler_params=params(40),
        cost_estimate=cost(10**10, 2 * 10**7),
        name="mesh_side",
    )(dst, halo, in_hbm(mesh_latent), in_hbm(enc_w), in_hbm(node_w), embed_out)

    slot = jnp.arange(cap, dtype=jnp.int32)[:, None]
    live = slot < g2m_count
    sums, halo_out = pl.pallas_call(
        encode,
        out_shape=(
            pltpu.HBM((mesh_rows * parts, 128), F32),
            pltpu.HBM((halo_slots, width), BF16),
        ),
        in_specs=[SMEM, SMEM, VMEM, ANY, ANY, ANY, VMEM, VMEM, ANY, ANY, ANY, VMEM],
        out_specs=(ANY, ANY),
        scratch_shapes=[
            scratch((mesh_rows + cap) * parts),
            scratch(slots, width, BF16),
            scratch(slots * parts),
            scratch(HALO_STEP * parts),
            scratch(HALO_STEP * parts),
            scratch(halo_slots, width, BF16),
            scratch(width, width, BF16),
            scratch(width, width, BF16),
            scratch(width, width, BF16),
            scratch(halo_slots, width, BF16),
            sems(6 + halo_slots // HALO_STEP // 2),
        ],
        compiler_params=params(32),
        name="encode",
    )(
        jnp.where(live, dst, mesh_rows + slot).T.reshape(-1) * parts, halo.T.reshape(-1) * parts, arrived, in_hbm(mesh_term), in_hbm(own),
        in_hbm(own_halo), embed_in, embed_centred, in_hbm(enc_w), folded, node_centred, gains,
    )
    halo_in = lax.all_to_all(
        halo_out.reshape(peers, halo_cap, width), axes, split_axis=0, concat_axis=0, tiled=True
    ).reshape(halo_slots, width)

    remote = proc_src >= mesh_rows
    mesh_new, local, proc_centred = pl.pallas_call(
        local_terms,
        out_shape=(
            pltpu.HBM((mesh_rows, width), BF16),
            pltpu.HBM((edges, width), BF16),
            pltpu.HBM((width, width), BF16),
        ),
        in_specs=[SMEM, SMEM, ANY, ANY, ANY, ANY, VMEM, ANY],
        out_specs=(ANY, ANY, VMEM),
        scratch_shapes=[
            scratch(mesh_rows * parts),
            scratch(mesh_rows, width, BF16),
            scratch(edges, width, BF16),
            scratch(mesh_rows, width, BF16),
            scratch(edges, width, BF16),
            scratch(width, width, BF16),
            pltpu.VMEM((4, width, width), BF16),
            scratch(mesh_rows * parts),
            scratch(mesh_rows * parts + 8),
            scratch(512 * parts),
            sems(2 + 2 * (mesh_rows // 512)),
            sems(2, edges // 512),
        ],
        compiler_params=params(40),
        cost_estimate=cost(2 * 10**10, 4 * 10**7),
        name="local_terms",
    )(
        proc_dst * parts,
        jnp.where(remote, mesh_rows, proc_src) * parts,
        in_hbm(sums),
        in_hbm(mesh_latent),
        node_centred,
        in_hbm(proc_w),
        gains,
        in_hbm(edge_latent),
    )
    edge_new = pl.pallas_call(
        edge_update,
        out_shape=pltpu.HBM((edges, width), BF16),
        in_specs=[SMEM, VMEM, ANY, ANY, ANY, ANY, VMEM],
        out_specs=ANY,
        scratch_shapes=[
            pltpu.VMEM((2, width, width), BF16),
            scratch(edges, width, BF16),
            scratch(edges, width, BF16),
            scratch(edges, width, BF16),
            scratch(halo_slots * parts + 8),
            scratch(EDGE_STEP * parts),
            scratch(EDGE_STEP * parts),
            sems(2),
            sems(2, edges // EDGE_STEP // 2),
        ],
        compiler_params=params(28),
        name="edge_update",
    )(
        jnp.where(remote, proc_src - mesh_rows, halo_slots) * parts,
        halo_in,
        in_hbm(proc_w),
        in_hbm(proc_centred),
        in_hbm(edge_latent),
        in_hbm(local),
        gains,
    )
    return (mesh_new, edge_new)


def solution(mesh):
    rows = P(("band", "tile"), None)
    slots = P(("band", "tile"), None, None)
    flat = P(("band", "tile"))
    in_specs = (
        rows, P(), P(), rows, rows, P(), P(), P(), P(), slots, slots, rows, slots, flat, flat,
    )
    return jax.shard_map(
        shards, mesh=mesh, in_specs=in_specs, out_specs=(rows, rows), check_vma=False
    )
```
